512 devices in a mesh: outer: 32 (over x, y, core), inner: 16 (over z).
Axes of the slice: x: 4, y: 4, z: 16, core: 2. Of those that a mesh axis runs over, the one named last changes fastest.
Arguments:
- right_side: float32 [256, 512, 128], P('outer', 'inner'), may hold values from -8 to 8
- codes: int32 [256, 512, 128], P('outer', 'inner'), may hold values from 0 to 7
Outputs:
- solution_field: float32 [256, 512, 128], P('outer', 'inner')
- residual: float32 [256, 512, 128], P('outer', 'inner')
The draws below stay inside these ranges and needn't reach their ends.
All inputs are finite; a program needn't handle non-finite values.
Results may differ from the reference program's by a relative error of at most 0.000062.
Values sent between devices are 32-bit elements; how exact they have to be, the bound alone decides.
No kernel may reach another device: no remote copies, remote signals or barrier semaphores. Data moves between devices by JAX's collectives and lax.ppermute only.
A program may use at most 64 MiB of HBM per device.

```python
import jax
import jax.numpy as jnp

CZ = 128
LEVELS = 4
NU_PRE = 2
NU_POST = 2
NU_COARSE = 6
NCODES = 8
NX = 256
NY = 512


def plant(array, key, least, top_value):
    place = [jax.random.randint(jax.random.fold_in(key, axis), (), 0, length) for axis, length in enumerate(array.shape)]
    longest = array.shape.index(max(array.shape))
    next_to = place[:longest] + [(place[longest] + 1) % array.shape[longest]] + place[longest + 1:]
    return array.at[tuple(place)].set(least).at[tuple(next_to)].set(top_value)


def block_levels(own_key, shape, cuts, low, largest):
    loudness, own = 1.0, jax.random.fold_in(own_key, 6)
    for dim, blocks in cuts:
        heights = jnp.exp(jax.random.uniform(jax.random.fold_in(own, dim), (blocks,), jnp.float32, low / len(cuts), largest / len(cuts)))
        loudness = loudness * jnp.repeat(heights, shape[dim] // blocks).reshape([-1 if axis == dim else 1 for axis in range(len(shape))])
    return loudness


def centred(own_key, shape, deviation, limit, split=(), kind=jnp.bfloat16):
    factor_of = block_levels(own_key, shape, split, -0.22, 0.18) if split else 1.0
    drawn = jax.random.normal(own_key, shape, jnp.float32) * deviation * factor_of
    return jnp.minimum(jnp.maximum(drawn, -limit), limit).astype(kind)


def setup_inputs(seed: int = 0) -> dict:
    key_of = jax.random.split(jax.random.key(seed), 3)
    right_side = centred(key_of[0], (NX, NY, CZ), 1.0, 8.0, ((0, 32), (1, 16)), jnp.float32)
    codes = plant(jax.random.randint(key_of[1], (NX, NY, CZ), 0, NCODES), jax.random.fold_in(key_of[1], 1), 0, NCODES - 1).astype(jnp.int32)
    return {"right_side": right_side, "codes": codes}


OMEGA = 0.8


def neighbours(ext, center):
    zeros = jnp.zeros_like(center[:, :, :1])
    return [ext[2:, 1:-1], ext[:-2, 1:-1], ext[1:-1, 2:], ext[1:-1, :-2],
            jnp.concatenate([center[:, :, 1:], zeros], axis=2),
            jnp.concatenate([zeros, center[:, :, :-1]], axis=2)]


def face_terms(kappa_ext, kappa):
    return [0.5 * (kappa + other) for other in neighbours(kappa_ext, kappa)]


def apply_op(ext, field, faces, scale):
    total = jnp.zeros_like(field)
    for face, other in zip(faces, neighbours(ext, field)):
        total = total + face * (field - other)
    return total * scale


def diagonal_of(faces, scale):
    total = jnp.zeros_like(faces[0])
    for face in faces:
        total = total + face
    return total * scale


def smooth(extend, field, source, faces, diag, scale, count):
    for sweep in range(count):
        field = field + OMEGA * (source - apply_op(extend(field), field, faces, scale)) / diag
    return field


def restrict(field):
    a, b, c = field.shape
    return field.reshape(a // 2, 2, b // 2, 2, c // 2, 2).mean(axis=(1, 3, 5))


def prolong(field):
    a, b, c = field.shape
    wide = jnp.broadcast_to(field[:, None, :, None, :, None], (a, 2, b, 2, c, 2))
    return wide.reshape(2 * a, 2 * b, 2 * c)


def padded(field):
    return jnp.pad(field, ((1, 1), (1, 1), (0, 0)))


def cycle(level, source, kappa):
    scale = 0.25 ** level
    faces = face_terms(padded(kappa), kappa)
    diag = diagonal_of(faces, scale)
    field = OMEGA * source / diag
    if level == LEVELS - 1:
        field = smooth(padded, field, source, faces, diag, scale, NU_COARSE - 1)
        leftover = source - apply_op(padded(field), field, faces, scale)
        ones = jnp.ones_like(field)
        weight = apply_op(padded(ones), ones, faces, scale)
        return field + jnp.sum(leftover) / jnp.sum(weight)
    field = smooth(padded, field, source, faces, diag, scale, NU_PRE - 1)
    remainder = source - apply_op(padded(field), field, faces, scale)
    correction = cycle(level + 1, restrict(remainder), restrict(kappa))
    field = field + prolong(correction)
    return smooth(padded, field, source, faces, diag, scale, NU_POST)


def reference(right_side, codes):
    kappa = jnp.exp(0.5 * codes.astype(jnp.float32))
    solution_field = cycle(0, right_side, kappa)
    faces = face_terms(padded(kappa), kappa)
    residual = right_side - apply_op(padded(solution_field), solution_field, faces, 1.0)
    return solution_field, residual
```

```python
import jax
import jax.numpy as jnp
from jax import lax
from jax.experimental import pallas as pl
from jax.experimental.pallas import tpu as pltpu
from jax.sharding import PartitionSpec as P


OMEGA = 0.8
F32 = jnp.float32
VMEM_LIMIT = 48 * 1024 * 1024


def iota(shape, dim):
    return lax.broadcasted_iota(jnp.int32, shape, dim)


def roll(x, shift, axis):
    return pltpu.roll(x, shift % x.shape[axis], axis)


def dot(a, b):
    return jnp.dot(a, b, precision=lax.Precision.HIGHEST, preferred_element_type=F32)


def lane_consts(rows, group, domain_rows=False):
    lane = iota((rows, 128), 1) % group
    zm = jnp.where(lane == group - 1, 0.0, 0.5).astype(F32)
    em = jnp.where((lane == 0) | (lane == group - 1), 0.5, 0.0).astype(F32)
    ym = None
    if domain_rows:
        row = iota((rows, 128), 0)
        ym = jnp.where(row == rows - 1, 0.0, 0.5).astype(F32)
        em = em + jnp.where((row == 0) | (row == rows - 1), 0.5, 0.0).astype(F32)
    return zm, em, ym


def make_faces(n, k, ax, ay, az, consts, inv=None, extra=None):
    zm, em, ym = consts

    def step(p, before):
        here = k[p]
        x = 0.5 * (here + k[p + 1])
        y = here + roll(here, -1, 0)
        y = 0.5 * y if ym is None else ym * y
        z = zm * (here + roll(here, -1, 1))
        ax[p] = x
        ay[p] = y
        az[p] = z
        if inv is not None:
            diag = em * here + x + before + y + roll(y, 1, 0) + z + roll(z, 1, 1)
            scaled = jnp.where(here > 0.0, OMEGA / diag, 0.0)
            inv[p] = scaled
            if extra is not None:
                extra(p, scaled)
        return x

    lax.fori_loop(0, n - 1, step, jnp.zeros(k.shape[1:], F32))


def apply_planes(first, last, v, k, ax, ay, az, consts, use, carry=None):
    em = consts[1]

    def step(p, state):
        before, carry = state
        here = v[p]
        x = ax[p] * (here - v[p + 1])
        y = ay[p] * (here - roll(here, -1, 0))
        z = az[p] * (here - roll(here, -1, 1))
        total = em * k[p] * here + (x - before) + (y - roll(y, 1, 0)) + (z - roll(z, 1, 1))
        return x, use(p, here, total, carry)

    start = ax[first - 1] * (v[first - 1] - v[first])
    return lax.fori_loop(first, last, step, (start, carry))[1]


def sweep(first, last, v, out, b, inv, k, ax, ay, az, consts):
    def use(p, here, total, _):
        out[p] = here + inv[p] * (b[p] - total)
        return 0

    apply_planes(first, last, v, k, ax, ay, az, consts, use, 0)


def ghosts(ref, n, width):
    lane = iota(ref.shape[1:], 1)
    ref[0] = jnp.where(lane < width, 0.0, roll(ref[n - 2], width, 1))
    ref[n - 1] = jnp.where(lane >= 128 - width, 0.0, roll(ref[1], -width, 1))


def pair_rows(tmp, x):
    half = x.shape[0] // 2
    tmp[...] = x
    return tmp[pl.ds(0, half, 2), :] + tmp[pl.ds(1, half, 2), :]


def twice_rows(tmp, x):
    n = x.shape[0]
    tmp[pl.ds(0, n, 2), :] = x
    tmp[pl.ds(1, n, 2), :] = x
    return tmp[...]


def gather_matrix(source, weight):
    return jnp.where(iota((128, 128), 0) == source(iota((128, 128), 1)), weight, 0.0).astype(F32)


def pair_matrix(target, weight):
    return jnp.where(iota((128, 128), 1) == target(iota((128, 128), 0)), weight, 0.0).astype(F32)


def prep_kernel(b_ref, codes_ref, low_ref, high_ref):
    kappa = jnp.exp(0.5 * codes_ref[...].astype(F32))
    low_ref[0] = kappa[:, :16]
    high_ref[0] = kappa[:, 16:]
    low_ref[1] = b_ref[:, :16]
    high_ref[1] = b_ref[:, 16:]


def fine_kernel(
    own_ref, even_ref, odd_ref,
    pay_ref, vb_ref, k1_ref, inv1_ref, k0_ref, b0_ref, v0_ref, inv0_ref,
    kb, ax, ay, az, inv, va, vb, tmp64, tmp32, s1, sk, b1, ax1, ay1, az1, va1, vb1, sems,
):
    right_first = lax.axis_index("outer") % 2 == 0

    @pl.when(right_first)
    def _():
        pltpu.make_async_copy(odd_ref, kb.at[:, pl.ds(0, 8)], sems.at[0]).start()
        pltpu.make_async_copy(even_ref, kb.at[:, pl.ds(16, 8)], sems.at[1]).start()

    @pl.when(jnp.logical_not(right_first))
    def _():
        pltpu.make_async_copy(even_ref, kb.at[:, pl.ds(0, 8)], sems.at[0]).start()
        pltpu.make_async_copy(odd_ref, kb.at[:, pl.ds(16, 8)], sems.at[1]).start()

    own = pltpu.make_async_copy(own_ref, kb.at[:, pl.ds(8, 8)], sems.at[2])
    own.start()
    pltpu.make_async_copy(odd_ref, kb.at[:, pl.ds(0, 8)], sems.at[0]).wait()
    pltpu.make_async_copy(odd_ref, kb.at[:, pl.ds(16, 8)], sems.at[1]).wait()
    own.wait()

    k, b = kb.at[0], kb.at[1]
    consts = lane_consts(64, 128)

    def first_sweep(p, scaled):
        va[p] = scaled * b[p]

    make_faces(24, k, ax, ay, az, consts, inv, first_sweep)
    sweep(2, 22, va, vb, b, inv, k, ax, ay, az, consts)

    def keep(p, _):
        k0_ref[p] = k[p + 4, pl.ds(8, 48), :]
        b0_ref[p] = b[p + 4, pl.ds(8, 48), :]
        v0_ref[p] = vb[p + 4, pl.ds(8, 48), :]
        inv0_ref[p] = inv[p + 4, pl.ds(8, 48), :]
        return 0

    lax.fori_loop(0, 16, keep, 0)

    def use(p, here, total, _):
        va[p] = b[p] - total
        return 0

    apply_planes(4, 20, vb, k, ax, ay, az, consts, use, 0)

    def coarsen_b(q, _):
        s1[pl.ds((q - 2) * 32, 32), :] = pair_rows(tmp64, va[2 * q] + va[2 * q + 1])
        return 0

    def coarsen_k(q, _):
        sk[pl.ds(q * 32, 32), :] = pair_rows(tmp64, k[2 * q] + k[2 * q + 1])
        return 0

    lax.fori_loop(2, 10, coarsen_b, 0)
    lax.fori_loop(0, 12, coarsen_k, 0)
    b1[pl.ds(2, 8)] = dot(s1[...], pair_matrix(lambda i: i // 2, 0.125)).reshape(8, 32, 128)
    k1_ref[...] = dot(sk[...], pair_matrix(lambda i: i // 2, 0.03125)).reshape(12, 32, 128)

    consts1 = lane_consts(32, 64)
    make_faces(12, k1_ref, ax1, ay1, az1, consts1, inv1_ref)
    va1[pl.ds(2, 8)] = inv1_ref[pl.ds(2, 8)] * b1[pl.ds(2, 8)]
    sweep(3, 9, va1, vb1, b1, inv1_ref, k1_ref, ax1, ay1, az1, consts1)

    def use1(p, here, total, _):
        va1[p] = b1[p] - total
        return 0

    apply_planes(4, 8, vb1, k1_ref, ax1, ay1, az1, consts1, use1, 0)
    for p in range(4):
        vb_ref[p] = vb1[4 + p] + roll(b1[4 + p], 64, 1)

    pay = jnp.zeros((16, 128), F32)
    for part, (field, weight) in enumerate(((va1, 0.125), (k1_ref, 0.03125))):
        for half in range(2):
            place = 64 * part + 32 * half
            rows = pair_rows(tmp32, field[4 + 2 * half] + field[5 + 2 * half])
            pay = pay + dot(rows, pair_matrix(lambda i: jnp.where(i < 64, place + i // 2, -1), weight))
    for i in range(32):
        pay_ref[i] = pay


def middle_kernel(
    all_ref, pay_ref, up_ref, down_ref, k_ref, inv_ref, b_ref, v_ref, ax, ay, az, va, vb, tmp16, s, sk
):
    group = iota((16, 128), 1) // 32
    for xl in range(16):
        for part, field in enumerate((b_ref, k_ref)):
            place = 2 * part + xl % 2
            plane = None
            for xh in range(4):
                block = all_ref[xl // 2 + 8 * xh]
                moved = block if xh == place else roll(block, 32 * (xh - place), 1)
                plane = moved if plane is None else jnp.where(group == xh, moved, plane)
            field[xl + 1] = plane
    ghosts(k_ref, 18, 32)
    consts = lane_consts(16, 32)
    inv_ref[0] = jnp.zeros((16, 128), F32)
    inv_ref[17] = jnp.zeros((16, 128), F32)
    b_ref[0] = jnp.zeros((16, 128), F32)
    b_ref[17] = jnp.zeros((16, 128), F32)

    def first_sweep(p, scaled):
        va[p] = scaled * b_ref[p]

    make_faces(18, k_ref, ax, ay, az, consts, inv_ref, first_sweep)
    ghosts(va, 18, 32)
    sweep(1, 17, va, v_ref, b_ref, inv_ref, k_ref, ax, ay, az, consts)
    ghosts(v_ref, 18, 32)

    def use(p, here, total, _):
        vb[p] = b_ref[p] - total
        return 0

    apply_planes(1, 17, v_ref, k_ref, ax, ay, az, consts, use, 0)
    for p in range(16):
        down_ref[p, 0:4] = v_ref[p + 1, 4:8, :]
        down_ref[p, 4:8] = b_ref[p + 1, 4:8, :]
        up_ref[p, 0:4] = v_ref[p + 1, 8:12, :]
        up_ref[p, 4:8] = b_ref[p + 1, 8:12, :]
    for t in range(8):
        s[t] = pair_rows(tmp16, vb[2 * t + 1] + vb[2 * t + 2])
        sk[t] = pair_rows(tmp16, k_ref[2 * t + 1] + k_ref[2 * t + 2])

    for part, (field, weight) in enumerate(((s, 0.125), (sk, 0.03125))):
        small = jnp.zeros((32, 128), F32)
        for u in range(2):
            m = pair_matrix(lambda i: (i // 32) * 32 + u * 16 + (i % 32) // 2, weight)
            small = small + dot(field[pl.ds(4 * u, 4)].reshape(32, 128), m)
        for t in range(4):
            vb[0, 4 * t : 4 * t + 4, :] = small[8 * t + 2 : 8 * t + 6, :]
        piece = vb[0]
        for i in range(16):
            pay_ref[i, 16 * part : 16 * part + 16, :] = piece


def coarse_kernel(
    all_ref, below_ref, above_ref, k2_ref, inv2_ref, b2_ref, v2_ref, vb1_ref, even_ref, odd_ref, k1_ref, inv1_ref,
    k0_any, b0_any, v0_any, inv0_any, v_out, r_out,
    k3, b3, ax3, ay3, az3, inv3, va3, vb3, c3, tmp16, ax2, ay2, az2, va2, vb2, b2,
    tmp32, s1, b1, va1, vb1, ax1, ay1, az1, tmp64, c1, k0, b0, v0, inv0, ax0, ay0, az0, w0, sems,
):
    outer, inner = lax.axis_index("outer"), lax.axis_index("inner")
    copies = [
        pltpu.make_async_copy(source, target, sems.at[i])
        for i, (source, target) in enumerate(((k0_any, k0), (b0_any, b0), (v0_any, v0), (inv0_any, inv0)))
    ]
    for copy in copies:
        copy.start()

    for i in range(16):
        for t in range(4):
            b3[t + 1, 4 * i : 4 * i + 4, :] = all_ref[i, 4 * t : 4 * t + 4, :]
            k3[t + 1, 4 * i : 4 * i + 4, :] = all_ref[i, 16 + 4 * t : 20 + 4 * t, :]
    ghosts(k3, 6, 16)
    b3[0] = jnp.zeros((64, 128), F32)
    consts3 = lane_consts(64, 16, True)

    def first_sweep(p, scaled):
        va3[p] = scaled * b3[p]

    make_faces(6, k3, ax3, ay3, az3, consts3, inv3, first_sweep)
    now, later = va3, vb3
    ghosts(now, 6, 16)
    for _ in range(5):
        sweep(1, 5, now, later, b3, inv3, k3, ax3, ay3, az3, consts3)
        now, later = later, now
        ghosts(now, 6, 16)

    def leftover(p, here, total, carry):
        return carry + (b3[p] - total)

    rest = apply_planes(1, 5, now, k3, ax3, ay3, az3, consts3, leftover, jnp.zeros((64, 128), F32))
    lane = iota((64, 128), 1)
    border = jnp.where(lane < 16, 0.5 * k3[1], 0.0) + jnp.where(lane >= 112, 0.5 * k3[4], 0.0)
    for p in range(1, 5):
        border = border + consts3[1] * k3[p]
    shift = jnp.sum(rest, keepdims=True) / jnp.sum(border, keepdims=True)
    for t in range(4):
        c3[t, 0:8, :] = jnp.zeros((8, 128), F32)
        c3[t, 8:72, :] = now[t + 1] + shift
        c3[t, 72:80, :] = jnp.zeros((8, 128), F32)

    near = jnp.concatenate([c3[t, pl.ds(4 * inner + 6, 8), :] for t in range(4)], axis=0)
    for u in range(2):
        wide = dot(near, gather_matrix(lambda j: (j // 32) * 32 + u * 16 + (j % 32) // 2, 1.0))
        for t in range(4):
            rows = twice_rows(tmp16, wide[8 * t : 8 * t + 8])
            for x in (2 * (4 * u + t), 2 * (4 * u + t) + 1):
                v2 = jnp.concatenate([below_ref[x, 0:4, :], v2_ref[x + 1, 4:12, :], above_ref[x, 0:4, :]], axis=0)
                b2[x + 1] = jnp.concatenate([below_ref[x, 4:8, :], b2_ref[x + 1, 4:12, :], above_ref[x, 4:8, :]], axis=0)
                va2[x + 1] = jnp.where(k2_ref[x + 1] > 0.0, v2 + rows, 0.0)
    consts2 = lane_consts(16, 32)
    make_faces(18, k2_ref, ax2, ay2, az2, consts2)
    ghosts(va2, 18, 32)
    sweep(1, 17, va2, vb2, b2, inv2_ref, k2_ref, ax2, ay2, az2, consts2)
    ghosts(vb2, 18, 32)
    sweep(1, 17, vb2, va2, b2, inv2_ref, k2_ref, ax2, ay2, az2, consts2)

    for q in range(6):
        x = lax.rem(2 * outer + 62 + q, 64)
        s1[pl.ds(16 * q, 16), :] = pltpu.roll(va2[lax.rem(x, 16) + 1], 128 - 32 * (x // 16), 1)
    wide = dot(s1[...], gather_matrix(lambda j: jnp.where(j < 64, j // 2, -1), 1.0))
    left_is_odd = outer % 2 == 0
    low = iota((32, 128), 1) < 64
    for q in range(6):
        rows = twice_rows(tmp32, wide[16 * q : 16 * q + 16])
        for p in (2 * q, 2 * q + 1):
            if p < 4:
                both = jnp.where(left_is_odd, odd_ref[p], even_ref[p])
            elif p < 8:
                both = vb1_ref[p - 4]
            else:
                both = jnp.where(left_is_odd, even_ref[p - 8], odd_ref[p - 8])
            b1[p] = roll(both, 64, 1)
            va1[p] = jnp.where(low & (k1_ref[p] > 0.0), both + rows, 0.0)
    consts1 = lane_consts(32, 64)
    make_faces(12, k1_ref, ax1, ay1, az1, consts1)
    sweep(1, 11, va1, vb1, b1, inv1_ref, k1_ref, ax1, ay1, az1, consts1)
    sweep(2, 10, vb1, va1, b1, inv1_ref, k1_ref, ax1, ay1, az1, consts1)

    c1[...] = dot(va1[pl.ds(2, 8)].reshape(256, 128), gather_matrix(lambda j: j // 2, 1.0))
    for copy in copies:
        copy.wait()

    def correct(q, _):
        twice_rows(tmp64, c1[pl.ds(32 * q, 32), :])
        rows = tmp64[pl.ds(8, 48), :]
        for p in (2 * q, 2 * q + 1):
            v0[p] = jnp.where(k0[p] > 0.0, v0[p] + rows, 0.0)
        return 0

    lax.fori_loop(0, 8, correct, 0)
    consts0 = lane_consts(48, 128)
    make_faces(16, k0, ax0, ay0, az0, consts0)
    sweep(2, 14, v0, w0, b0, inv0, k0, ax0, ay0, az0, consts0)
    sweep(3, 13, w0, v0, b0, inv0, k0, ax0, ay0, az0, consts0)

    def use(p, here, total, _):
        v_out[p - 4] = here[8:40]
        r_out[p - 4] = (b0[p] - total)[8:40]
        return 0

    apply_planes(4, 12, v0, k0, ax0, ay0, az0, consts0, use, 0)


def vmem(*shape):
    return pltpu.VMEM(shape, F32)


def out(*shape):
    return jax.ShapeDtypeStruct(shape, F32)


def call(kernel, name, ins, outs, scratch, args):
    spec = {"v": pl.BlockSpec(memory_space=pltpu.VMEM), "a": pl.BlockSpec(memory_space=pl.ANY)}
    return pl.pallas_call(
        kernel,
        name=name,
        out_shape=outs,
        in_specs=[spec[c] for c in ins],
        out_specs=[spec["v"]] * len(outs),
        scratch_shapes=scratch,
        compiler_params=pltpu.CompilerParams(vmem_limit_bytes=VMEM_LIMIT),
    )(*args)


def body(right_side, codes):
    groups, boxes = lax.axis_size("outer"), lax.axis_size("inner")
    evens = [(i, i ^ 1) for i in range(groups)]
    odds = [(i, ((i + 1) ^ 1) - 1) for i in range(1, groups - 1)]
    ups = [(i, i + 1) for i in range(boxes - 1)]
    downs = [(i + 1, i) for i in range(boxes - 1)]

    low, high = call(prep_kernel, "prep", "vv", [out(2, 8, 16, 128)] * 2, [], (right_side, codes))
    below = lax.ppermute(high, "inner", ups)
    above = lax.ppermute(low, "inner", downs)
    own = jnp.concatenate([below, low, high, above], axis=2)
    even = lax.ppermute(own, "outer", evens)
    odd = lax.ppermute(own, "outer", odds)

    fine, level1 = (24, 64, 128), (12, 32, 128)
    pay, vb1, k1, inv1, k0, b0, v0, inv0 = call(
        fine_kernel, "fine", "aaa",
        [out(32, 16, 128), out(4, 32, 128), out(*level1), out(*level1)] + [out(16, 48, 128)] * 4,
        [vmem(2, *fine)] + [vmem(*fine)] * 6 + [vmem(64, 128), vmem(32, 128), vmem(256, 128), vmem(384, 128)]
        + [vmem(*level1)] * 6 + [pltpu.SemaphoreType.DMA((3,))],
        (own, even, odd),
    )
    even1 = lax.ppermute(vb1, "outer", evens)
    odd1 = lax.ppermute(vb1, "outer", odds)
    slab = lax.all_to_all(pay, "outer", 0, 0, tiled=True)

    level2 = (18, 16, 128)
    pay3, up, down, k2, inv2, b2, v2 = call(
        middle_kernel, "middle", "v",
        [out(16, 32, 128), out(16, 8, 128), out(16, 8, 128)] + [out(*level2)] * 4,
        [vmem(*level2)] * 5 + [vmem(16, 128), vmem(8, 8, 128), vmem(8, 8, 128)],
        (slab,),
    )
    below2 = lax.ppermute(up, "inner", ups)
    above2 = lax.ppermute(down, "inner", downs)
    whole = lax.all_to_all(pay3, "inner", 0, 0, tiled=True)

    level3, window = (6, 64, 128), (16, 48, 128)
    return call(
        coarse_kernel, "coarse", "v" * 12 + "a" * 4,
        [out(8, 32, 128)] * 2,
        [vmem(*level3)] * 8 + [vmem(4, 80, 128), vmem(16, 128)] + [vmem(*level2)] * 6
        + [vmem(32, 128), vmem(96, 128)] + [vmem(*level1)] * 6 + [vmem(64, 128), vmem(256, 128)]
        + [vmem(*window)] * 8 + [pltpu.SemaphoreType.DMA((4,))],
        (whole, below2, above2, k2, inv2, b2, v2, vb1, even1, odd1, k1, inv1, k0, b0, v0, inv0),
    )


def solution(mesh):
    placed = P("outer", "inner", None)
    return jax.shard_map(
        lambda right_side, codes: tuple(body(right_side, codes)),
        mesh=mesh,
        in_specs=(placed, placed),
        out_specs=(placed, placed),
        check_vma=False,
    )
```

```python
import jax
import jax.numpy as jnp
from jax import lax
from jax.experimental import pallas as pl
from jax.experimental.pallas import tpu as pltpu
from jax.sharding import PartitionSpec as P


OMEGA = 0.8
F32 = jnp.float32
VMEM_LIMIT = 24 * 1024 * 1024
UNROLL = 96


def iota(shape, dim):
    return lax.broadcasted_iota(jnp.int32, shape, dim)


def roll(x, shift, axis):
    return pltpu.roll(x, shift % x.shape[axis], axis)


def dot(a, b):
    return jnp.dot(a, b, precision=lax.Precision.HIGHEST, preferred_element_type=F32)


def lane_consts(rows, group, domain_rows=False):
    lane = iota((rows, 128), 1) % group
    zm = jnp.where(lane == group - 1, 0.0, 0.5).astype(F32)
    em = jnp.where((lane == 0) | (lane == group - 1), 0.5, 0.0).astype(F32)
    ym = None
    if domain_rows:
        row = iota((rows, 128), 0)
        ym = jnp.where(row == rows - 1, 0.0, 0.5).astype(F32)
        em = em + jnp.where((row == 0) | (row == rows - 1), 0.5, 0.0).astype(F32)
    return zm, em, ym


def loop(first, last, rows, step, carry):
    count = last - first
    width = max(1, min(count, UNROLL // (rows // 8)))
    whole = count // width

    def block(i, carry):
        for u in range(width):
            carry = step(first + i * width + u, carry)
        return carry

    if whole == 1:
        carry = block(0, carry)
    else:
        carry = lax.fori_loop(0, whole, block, carry)
    for p in range(first + whole * width, last):
        carry = step(p, carry)
    return carry


def make_faces(n, k, ax, ay, az, consts, inv=None, extra=None):
    zm, em, ym = consts

    def step(p, before):
        here = k[p]
        x = 0.5 * (here + k[p + 1])
        y = here + roll(here, -1, 0)
        y = 0.5 * y if ym is None else ym * y
        z = zm * (here + roll(here, -1, 1))
        ax[p] = x
        ay[p] = y
        az[p] = z
        if inv is not None:
            diag = em * here + x + before + y + roll(y, 1, 0) + z + roll(z, 1, 1)
            scaled = jnp.where(here > 0.0, OMEGA / diag, 0.0)
            inv[p] = scaled
            if extra is not None:
                extra(p, scaled)
        return x

    loop(0, n - 1, k.shape[1], step, jnp.zeros(k.shape[1:], F32))


def apply_planes(first, last, v, k, ax, ay, az, consts, use, carry=None):
    em = consts[1]

    def step(p, state):
        before, carry = state
        here = v[p]
        x = ax[p] * (here - v[p + 1])
        y = ay[p] * (here - roll(here, -1, 0))
        z = az[p] * (here - roll(here, -1, 1))
        total = em * k[p] * here + (x - before) + (y - roll(y, 1, 0)) + (z - roll(z, 1, 1))
        return x, use(p, here, total, carry)

    start = ax[first - 1] * (v[first - 1] - v[first])
    return loop(first, last, v.shape[1], step, (start, carry))[1]


def sweep(first, last, v, out, b, inv, k, ax, ay, az, consts):
    def use(p, here, total, _):
        out[p] = here + inv[p] * (b[p] - total)
        return 0

    apply_planes(first, last, v, k, ax, ay, az, consts, use, 0)


def ghosts(ref, n, width):
    lane = iota(ref.shape[1:], 1)
    ref[0] = jnp.where(lane < width, 0.0, roll(ref[n - 2], width, 1))
    ref[n - 1] = jnp.where(lane >= 128 - width, 0.0, roll(ref[1], -width, 1))


def pair_rows(tmp, x):
    half = x.shape[0] // 2
    tmp[...] = x
    return tmp[pl.ds(0, half, 2), :] + tmp[pl.ds(1, half, 2), :]


def twice_rows(tmp, x):
    n = x.shape[0]
    tmp[pl.ds(0, n, 2), :] = x
    tmp[pl.ds(1, n, 2), :] = x
    return tmp[...]


def gather_matrix(source, weight):
    return jnp.where(iota((128, 128), 0) == source(iota((128, 128), 1)), weight, 0.0).astype(F32)


def pair_matrix(target, weight):
    return jnp.where(iota((128, 128), 1) == target(iota((128, 128), 0)), weight, 0.0).astype(F32)


def prep_kernel(b_ref, codes_ref, low_ref, high_ref):
    kappa = jnp.exp(0.5 * codes_ref[...].astype(F32))
    low_ref[0] = kappa[:, :16]
    high_ref[0] = kappa[:, 16:]
    low_ref[1] = b_ref[:, :16]
    high_ref[1] = b_ref[:, 16:]


def fine_kernel(
    own_ref, even_ref, odd_ref,
    pay_ref, vb_ref, k1_ref, inv1_ref, k0_ref, b0_ref, v0_ref, inv0_ref,
    kb, ax, ay, az, inv, va, vb, tmp64, tmp32, s1, sk, b1, ax1, ay1, az1, va1, vb1, sems,
):
    right_first = lax.axis_index("outer") % 2 == 0

    @pl.when(right_first)
    def _():
        pltpu.make_async_copy(odd_ref, kb.at[:, pl.ds(0, 8)], sems.at[0]).start()
        pltpu.make_async_copy(even_ref, kb.at[:, pl.ds(16, 8)], sems.at[1]).start()

    @pl.when(jnp.logical_not(right_first))
    def _():
        pltpu.make_async_copy(even_ref, kb.at[:, pl.ds(0, 8)], sems.at[0]).start()
        pltpu.make_async_copy(odd_ref, kb.at[:, pl.ds(16, 8)], sems.at[1]).start()

    own = pltpu.make_async_copy(own_ref, kb.at[:, pl.ds(8, 8)], sems.at[2])
    own.start()
    pltpu.make_async_copy(odd_ref, kb.at[:, pl.ds(0, 8)], sems.at[0]).wait()
    pltpu.make_async_copy(odd_ref, kb.at[:, pl.ds(16, 8)], sems.at[1]).wait()
    own.wait()

    k, b = kb.at[0], kb.at[1]
    consts = lane_consts(64, 128)

    def first_sweep(p, scaled):
        va[p] = scaled * b[p]

    make_faces(24, k, ax, ay, az, consts, inv, first_sweep)
    sweep(2, 22, va, vb, b, inv, k, ax, ay, az, consts)

    def keep(p, _):
        k0_ref[p] = k[p + 4, pl.ds(8, 48), :]
        b0_ref[p] = b[p + 4, pl.ds(8, 48), :]
        v0_ref[p] = vb[p + 4, pl.ds(8, 48), :]
        inv0_ref[p] = inv[p + 4, pl.ds(8, 48), :]
        return 0

    loop(0, 16, 32, keep, 0)

    def use(p, here, total, _):
        va[p] = b[p] - total
        return 0

    apply_planes(4, 20, vb, k, ax, ay, az, consts, use, 0)

    def coarsen_b(q, _):
        s1[pl.ds((q - 2) * 32, 32), :] = pair_rows(tmp64, va[2 * q] + va[2 * q + 1])
        return 0

    def coarsen_k(q, _):
        sk[pl.ds(q * 32, 32), :] = pair_rows(tmp64, k[2 * q] + k[2 * q + 1])
        return 0

    loop(2, 10, 64, coarsen_b, 0)
    loop(0, 12, 64, coarsen_k, 0)
    b1[pl.ds(2, 8)] = dot(s1[...], pair_matrix(lambda i: i // 2, 0.125)).reshape(8, 32, 128)
    k1_ref[...] = dot(sk[...], pair_matrix(lambda i: i // 2, 0.03125)).reshape(12, 32, 128)

    consts1 = lane_consts(32, 64)
    make_faces(12, k1_ref, ax1, ay1, az1, consts1, inv1_ref)
    va1[pl.ds(2, 8)] = inv1_ref[pl.ds(2, 8)] * b1[pl.ds(2, 8)]
    sweep(3, 9, va1, vb1, b1, inv1_ref, k1_ref, ax1, ay1, az1, consts1)

    def use1(p, here, total, _):
        va1[p] = b1[p] - total
        return 0

    apply_planes(4, 8, vb1, k1_ref, ax1, ay1, az1, consts1, use1, 0)
    for p in range(4):
        vb_ref[p] = vb1[4 + p] + roll(b1[4 + p], 64, 1)

    pay = jnp.zeros((16, 128), F32)
    for part, (field, weight) in enumerate(((va1, 0.125), (k1_ref, 0.03125))):
        for half in range(2):
            place = 64 * part + 32 * half
            rows = pair_rows(tmp32, field[4 + 2 * half] + field[5 + 2 * half])
            pay = pay + dot(rows, pair_matrix(lambda i: jnp.where(i < 64, place + i // 2, -1), weight))
    for i in range(32):
        pay_ref[i] = pay


def middle_kernel(
    all_ref, _even1, _odd1, pay_ref, up_ref, down_ref, kw_ref, invw_ref, bw_ref, vw_ref,
    k_ref, inv_ref, b_ref, v_ref, ax, ay, az, va, vb, tmp16, s, sk,
):
    group = iota((16, 128), 1) // 32
    for xl in range(16):
        for part, field in enumerate((b_ref, k_ref)):
            place = 2 * part + xl % 2
            plane = None
            for xh in range(4):
                block = all_ref[xl // 2 + 8 * xh]
                moved = block if xh == place else roll(block, 32 * (xh - place), 1)
                plane = moved if plane is None else jnp.where(group == xh, moved, plane)
            field[xl + 1] = plane
    ghosts(k_ref, 18, 32)
    consts = lane_consts(16, 32)
    inv_ref[0] = jnp.zeros((16, 128), F32)
    inv_ref[17] = jnp.zeros((16, 128), F32)
    b_ref[0] = jnp.zeros((16, 128), F32)
    b_ref[17] = jnp.zeros((16, 128), F32)

    def first_sweep(p, scaled):
        va[p] = scaled * b_ref[p]

    make_faces(18, k_ref, ax, ay, az, consts, inv_ref, first_sweep)
    ghosts(va, 18, 32)
    sweep(1, 17, va, v_ref, b_ref, inv_ref, k_ref, ax, ay, az, consts)
    ghosts(v_ref, 18, 32)

    def use(p, here, total, _):
        vb[p] = b_ref[p] - total
        return 0

    apply_planes(1, 17, v_ref, k_ref, ax, ay, az, consts, use, 0)
    first = 2 * lax.axis_index("outer") + 60
    near = []
    for q in range(10):
        x = lax.rem(first + q, 64)
        place = lax.rem(x, 16) + 1
        back = lax.rem(128 - 32 * (x // 16), 128)
        kept = (group == 0) & (first + q >= 64) & (first + q < 128)
        for field, window in ((k_ref, kw_ref), (inv_ref, invw_ref), (b_ref, bw_ref), (v_ref, vw_ref)):
            window[q] = jnp.where(kept, pltpu.roll(field[place], back, 1), 0.0)
        near.append(vw_ref[q] + roll(bw_ref[q], 32, 1))
    for q in range(5):
        both = near[q] + roll(near[q + 5], 64, 1)
        down_ref[4 * q : 4 * q + 4, :] = both[4:8]
        up_ref[4 * q : 4 * q + 4, :] = both[8:12]
    for t in range(8):
        s[t] = pair_rows(tmp16, vb[2 * t + 1] + vb[2 * t + 2])
        sk[t] = pair_rows(tmp16, k_ref[2 * t + 1] + k_ref[2 * t + 2])

    for part, (field, weight) in enumerate(((s, 0.125), (sk, 0.03125))):
        small = jnp.zeros((32, 128), F32)
        for u in range(2):
            m = pair_matrix(lambda i: (i // 32) * 32 + u * 16 + (i % 32) // 2, weight)
            small = small + dot(field[pl.ds(4 * u, 4)].reshape(32, 128), m)
        for t in range(4):
            vb[0, 4 * t : 4 * t + 4, :] = small[8 * t + 2 : 8 * t + 6, :]
        piece = vb[0]
        for i in range(16):
            pay_ref[i, 16 * part : 16 * part + 16, :] = piece


def coarse_kernel(
    all_ref, below_ref, above_ref, k2_ref, inv2_ref, b2_ref, v2_ref, vb1_ref, even_ref, odd_ref, k1_ref, inv1_ref,
    k0, b0, v0_ref, inv0, v_out, r_out,
    k3, b3, ax3, ay3, az3, inv3, va3, vb3, c3, tmp16, ax2, ay2, az2, va2, vb2, b2,
    tmp32, b1, va1, vb1, ax1, ay1, az1, tmp64, c1, v0, ax0, ay0, az0, w0,
):
    outer, inner = lax.axis_index("outer"), lax.axis_index("inner")
    for i in range(16):
        for t in range(4):
            b3[t + 1, 4 * i : 4 * i + 4, :] = all_ref[i, 4 * t : 4 * t + 4, :]
            k3[t + 1, 4 * i : 4 * i + 4, :] = all_ref[i, 16 + 4 * t : 20 + 4 * t, :]
    ghosts(k3, 6, 16)
    b3[0] = jnp.zeros((64, 128), F32)
    consts3 = lane_consts(64, 16, True)

    def first_sweep(p, scaled):
        va3[p] = scaled * b3[p]

    make_faces(6, k3, ax3, ay3, az3, consts3, inv3, first_sweep)
    now, later = va3, vb3
    ghosts(now, 6, 16)
    for _ in range(5):
        sweep(1, 5, now, later, b3, inv3, k3, ax3, ay3, az3, consts3)
        now, later = later, now
        ghosts(now, 6, 16)

    def leftover(p, here, total, carry):
        return carry + (b3[p] - total)

    rest = apply_planes(1, 5, now, k3, ax3, ay3, az3, consts3, leftover, jnp.zeros((64, 128), F32))
    lane = iota((64, 128), 1)
    border = jnp.where(lane < 16, 0.5 * k3[1], 0.0) + jnp.where(lane >= 112, 0.5 * k3[4], 0.0)
    for p in range(1, 5):
        border = border + consts3[1] * k3[p]
    shift = jnp.sum(rest, keepdims=True) / jnp.sum(border, keepdims=True)
    for t in range(4):
        c3[t, 0:8, :] = jnp.zeros((8, 128), F32)
        c3[t, 8:72, :] = now[t + 1] + shift
        c3[t, 72:80, :] = jnp.zeros((8, 128), F32)

    near = []
    for q in range(5):
        x = lax.rem(outer + 30 + q, 32)
        back = lax.rem(128 - 16 * (x // 4), 128)
        near.append(pltpu.roll(c3[lax.rem(x, 4), pl.ds(4 * inner + 6, 8), :], back, 1))
    wide = dot(jnp.concatenate(near, axis=0), gather_matrix(lambda j: jnp.where(j < 32, j // 2, -1), 1.0))
    lane = iota((16, 128), 1)
    for q in range(10):
        rows = twice_rows(tmp16, wide[8 * (q // 2) : 8 * (q // 2) + 8])
        below, above = (ref[4 * (q % 5) : 4 * (q % 5) + 4, :] for ref in (below_ref, above_ref))
        if q >= 5:
            below, above = roll(below, 64, 1), roll(above, 64, 1)
        v2 = jnp.concatenate([below, v2_ref[q, 4:12, :], above], axis=0)
        b2[q] = jnp.concatenate([roll(below, 96, 1), b2_ref[q, 4:12, :], roll(above, 96, 1)], axis=0)
        va2[q] = jnp.where((lane < 32) & (k2_ref[q] > 0.0), v2 + rows, 0.0)
    consts2 = lane_consts(16, 32)
    make_faces(10, k2_ref, ax2, ay2, az2, consts2)
    sweep(1, 9, va2, vb2, b2, inv2_ref, k2_ref, ax2, ay2, az2, consts2)
    sweep(2, 8, vb2, va2, b2, inv2_ref, k2_ref, ax2, ay2, az2, consts2)

    wide = dot(va2[pl.ds(2, 6)].reshape(96, 128), gather_matrix(lambda j: jnp.where(j < 64, j // 2, -1), 1.0))
    left_is_odd = outer % 2 == 0
    low = iota((32, 128), 1) < 64
    for q in range(6):
        rows = twice_rows(tmp32, wide[16 * q : 16 * q + 16])
        for p in (2 * q, 2 * q + 1):
            if p < 4:
                both = jnp.where(left_is_odd, odd_ref[p], even_ref[p])
            elif p < 8:
                both = vb1_ref[p - 4]
            else:
                both = jnp.where(left_is_odd, even_ref[p - 8], odd_ref[p - 8])
            b1[p] = roll(both, 64, 1)
            va1[p] = jnp.where(low & (k1_ref[p] > 0.0), both + rows, 0.0)
    consts1 = lane_consts(32, 64)
    make_faces(12, k1_ref, ax1, ay1, az1, consts1)
    sweep(1, 11, va1, vb1, b1, inv1_ref, k1_ref, ax1, ay1, az1, consts1)
    sweep(2, 10, vb1, va1, b1, inv1_ref, k1_ref, ax1, ay1, az1, consts1)

    c1[...] = dot(va1[pl.ds(2, 8)].reshape(256, 128), gather_matrix(lambda j: j // 2, 1.0))

    def correct(q, _):
        twice_rows(tmp64, c1[pl.ds(32 * q, 32), :])
        rows = tmp64[pl.ds(8, 48), :]
        for p in (2 * q, 2 * q + 1):
            v0[p] = jnp.where(k0[p] > 0.0, v0_ref[p] + rows, 0.0)
        return 0

    loop(0, 8, 64, correct, 0)
    consts0 = lane_consts(48, 128)
    make_faces(16, k0, ax0, ay0, az0, consts0)
    sweep(2, 14, v0, w0, b0, inv0, k0, ax0, ay0, az0, consts0)
    sweep(3, 13, w0, v0, b0, inv0, k0, ax0, ay0, az0, consts0)

    def use(p, here, total, _):
        v_out[p - 4] = here[8:40]
        r_out[p - 4] = (b0[p] - total)[8:40]
        return 0

    apply_planes(4, 12, v0, k0, ax0, ay0, az0, consts0, use, 0)


def vmem(*shape):
    return pltpu.VMEM(shape, F32)


def out(*shape):
    return jax.ShapeDtypeStruct(shape, F32)


def call(kernel, name, ins, outs, scratch, args):
    spec = {"v": pl.BlockSpec(memory_space=pltpu.VMEM), "a": pl.BlockSpec(memory_space=pl.ANY)}
    return pl.pallas_call(
        kernel,
        name=name,
        out_shape=outs,
        in_specs=[spec[c] for c in ins],
        out_specs=[spec["v"]] * len(outs),
        scratch_shapes=scratch,
        compiler_params=pltpu.CompilerParams(vmem_limit_bytes=VMEM_LIMIT),
    )(*args)


def body(right_side, codes):
    groups, boxes = lax.axis_size("outer"), lax.axis_size("inner")
    evens = [(i, i ^ 1) for i in range(groups)]
    odds = [(i, ((i + 1) ^ 1) - 1) for i in range(1, groups - 1)]
    ups = [(i, i + 1) for i in range(boxes - 1)]
    downs = [(i + 1, i) for i in range(boxes - 1)]

    low, high = call(prep_kernel, "prep", "vv", [out(2, 8, 16, 128)] * 2, [], (right_side, codes))
    below = lax.ppermute(high, "inner", ups)
    above = lax.ppermute(low, "inner", downs)
    own = jnp.concatenate([below, low, high, above], axis=2)
    even = lax.ppermute(own, "outer", evens)
    odd = lax.ppermute(own, "outer", odds)

    fine, level1 = (24, 64, 128), (12, 32, 128)
    pay, vb1, k1, inv1, k0, b0, v0, inv0 = call(
        fine_kernel, "fine", "aaa",
        [out(32, 16, 128), out(4, 32, 128), out(*level1), out(*level1)] + [out(16, 48, 128)] * 4,
        [vmem(2, *fine)] + [vmem(*fine)] * 6 + [vmem(64, 128), vmem(32, 128), vmem(256, 128), vmem(384, 128)]
        + [vmem(*level1)] * 6 + [pltpu.SemaphoreType.DMA((3,))],
        (own, even, odd),
    )
    even1 = lax.ppermute(vb1, "outer", evens)
    odd1 = lax.ppermute(vb1, "outer", odds)
    slab = lax.all_to_all(pay, "outer", 0, 0, tiled=True)

    level2, window2 = (18, 16, 128), (10, 16, 128)
    pay3, up, down, k2, inv2, b2, v2 = call(
        middle_kernel, "middle", "vaa",
        [out(16, 32, 128), out(24, 128), out(24, 128)] + [out(*window2)] * 4,
        [vmem(*level2)] * 9 + [vmem(16, 128), vmem(8, 8, 128), vmem(8, 8, 128)],
        (slab, even1, odd1),
    )
    below2 = lax.ppermute(up, "inner", ups)
    above2 = lax.ppermute(down, "inner", downs)
    whole = lax.all_to_all(pay3, "inner", 0, 0, tiled=True)

    level3, window = (6, 64, 128), (16, 48, 128)
    return call(
        coarse_kernel, "coarse", "v" * 16,
        [out(8, 32, 128)] * 2,
        [vmem(*level3)] * 8 + [vmem(4, 80, 128), vmem(16, 128)] + [vmem(*window2)] * 6
        + [vmem(32, 128)] + [vmem(*level1)] * 6 + [vmem(64, 128), vmem(256, 128)]
        + [vmem(*window)] * 5,
        (whole, below2, above2, k2, inv2, b2, v2, vb1, even1, odd1, k1, inv1, k0, b0, v0, inv0),
    )


def solution(mesh):
    placed = P("outer", "inner", None)
    return jax.shard_map(
        lambda right_side, codes: tuple(body(right_side, codes)),
        mesh=mesh,
        in_specs=(placed, placed),
        out_specs=(placed, placed),
        check_vma=False,
    )
```

```python
import jax
import jax.numpy as jnp
from jax import lax
from jax.experimental import pallas as pl
from jax.experimental.pallas import tpu as pltpu
from jax.sharding import PartitionSpec as P


OMEGA = 0.8
F32 = jnp.float32
VMEM_LIMIT = 24 * 1024 * 1024
UNROLL = 96


def iota(shape, dim):
    return lax.broadcasted_iota(jnp.int32, shape, dim)


def roll(x, shift, axis):
    return pltpu.roll(x, shift % x.shape[axis], axis)


def dot(a, b):
    return jnp.dot(a, b, precision=lax.Precision.HIGHEST, preferred_element_type=F32)


def lane_consts(rows, group, domain_rows=False):
    lane = iota((rows, 128), 1) % group
    zm = jnp.where(lane == group - 1, 0.0, 0.5).astype(F32)
    em = jnp.where((lane == 0) | (lane == group - 1), 0.5, 0.0).astype(F32)
    ym = None
    if domain_rows:
        row = iota((rows, 128), 0)
        ym = jnp.where(row == rows - 1, 0.0, 0.5).astype(F32)
        em = em + jnp.where((row == 0) | (row == rows - 1), 0.5, 0.0).astype(F32)
    return zm, em, ym


def loop(first, last, rows, step, carry):
    count = last - first
    width = max(1, min(count, UNROLL // (rows // 8)))
    whole = count // width

    def block(i, carry):
        for u in range(width):
            carry = step(first + i * width + u, carry)
        return carry

    if whole == 1:
        carry = block(0, carry)
    else:
        carry = lax.fori_loop(0, whole, block, carry)
    for p in range(first + whole * width, last):
        carry = step(p, carry)
    return carry


def make_faces(n, k, ax, ay, az, consts, inv=None, extra=None):
    zm, em, ym = consts

    def step(p, before):
        here = k[p]
        x = 0.5 * (here + k[p + 1])
        y = here + roll(here, -1, 0)
        y = 0.5 * y if ym is None else ym * y
        z = zm * (here + roll(here, -1, 1))
        ax[p] = x
        ay[p] = y
        az[p] = z
        if inv is not None:
            diag = em * here + x + before + y + roll(y, 1, 0) + z + roll(z, 1, 1)
            scaled = jnp.where(here > 0.0, OMEGA / diag, 0.0)
            inv[p] = scaled
            if extra is not None:
                extra(p, scaled)
        return x

    loop(0, n - 1, k.shape[1], step, jnp.zeros(k.shape[1:], F32))


def apply_planes(first, last, v, k, ax, ay, az, consts, use, carry=None):
    em = consts[1]

    def step(p, state):
        before, carry = state
        here = v[p]
        x = ax[p] * (here - v[p + 1])
        y = ay[p] * (here - roll(here, -1, 0))
        z = az[p] * (here - roll(here, -1, 1))
        total = em * k[p] * here + (x - before) + (y - roll(y, 1, 0)) + (z - roll(z, 1, 1))
        return x, use(p, here, total, carry)

    start = ax[first - 1] * (v[first - 1] - v[first])
    return loop(first, last, v.shape[1], step, (start, carry))[1]


def sweep(first, last, v, out, b, inv, k, ax, ay, az, consts):
    def use(p, here, total, _):
        out[p] = here + inv[p] * (b[p] - total)
        return 0

    apply_planes(first, last, v, k, ax, ay, az, consts, use, 0)


def ghosts(ref, n, width):
    lane = iota(ref.shape[1:], 1)
    ref[0] = jnp.where(lane < width, 0.0, roll(ref[n - 2], width, 1))
    ref[n - 1] = jnp.where(lane >= 128 - width, 0.0, roll(ref[1], -width, 1))


def pair_rows(tmp, x):
    half = x.shape[0] // 2
    tmp[...] = x
    return tmp[pl.ds(0, half, 2), :] + tmp[pl.ds(1, half, 2), :]


def twice_rows(tmp, x):
    n = x.shape[0]
    tmp[pl.ds(0, n, 2), :] = x
    tmp[pl.ds(1, n, 2), :] = x
    return tmp[...]


def gather_matrix(source, weight):
    return jnp.where(iota((128, 128), 0) == source(iota((128, 128), 1)), weight, 0.0).astype(F32)


def pair_matrix(target, weight):
    return jnp.where(iota((128, 128), 1) == target(iota((128, 128), 0)), weight, 0.0).astype(F32)


def prep_kernel(b_ref, codes_ref, even_ref, odd_ref):
    kappa = jnp.exp(0.5 * codes_ref[...].astype(F32))
    up_first = lax.axis_index("inner") % 2 == 0
    for part, field in enumerate((kappa, b_ref[...])):
        low, high = field[:, :16], field[:, 16:]
        even_ref[part] = jnp.where(up_first, high, low)
        odd_ref[part] = jnp.where(up_first, low, high)


SENT = [(0, d, 16 if d <= 6 else 8) for d in range(1, 9)] + [(1, d, 16 if d <= 5 else 8) for d in range(1, 7)]
SENT_ROWS = sum(32 + 2 * halo for _, _, halo in SENT)


def sent_places():
    first = 0
    for field, d, halo in SENT:
        yield field, d, halo, first
        first += 32 + 2 * halo


def in_order(refs):
    even_ref, odd_ref, from_even_ref, from_odd_ref = refs
    up_first = lax.axis_index("inner") % 2 == 0

    def group(i, *place):
        one, other = ((from_odd_ref, from_even_ref), (odd_ref, even_ref), (even_ref, odd_ref), (from_even_ref, from_odd_ref))[i]
        return jnp.where(up_first, one[place], other[place])

    return group


def pack_kernel(*refs):
    group, out_ref = in_order(refs[:4]), refs[4]
    right = lax.axis_index("outer") % 2 == 1
    for field, d, halo, first in sent_places():
        plane = jnp.where(right, 8 - d, d - 1)
        rows = [group(i, field, plane) for i in range(4)]
        rows[0], rows[3] = rows[0][16 - halo :], rows[3][:halo]
        for part in rows:
            out_ref[first : first + part.shape[0], :] = part
            first += part.shape[0]


def join_kernel(*refs):
    group = in_order(refs[:4])
    for field, own_ref in enumerate(refs[5:]):
        for p in range(8):
            for i in range(4):
                own_ref[p, 16 * i : 16 * i + 16, :] = group(i, field, p)


def fine_kernel(
    kappas_ref, sources_ref, odd_ref,
    pay_ref, vb_ref, k1_ref, inv1_ref, k0_ref, b0_ref, v0_ref, inv0_ref,
    kb, ax, ay, az, inv, va, vb, tmp64, tmp32, s1, sk, b1, ax1, ay1, az1, va1, vb1,
):
    core = lax.axis_index("outer") % 2
    right_first = core == 0
    chip_first = jnp.where(right_first, 8, 0)
    zeros = jnp.zeros((64, 128), F32)
    for field, far in ((0, (7, 8)), (1, (6, 7, 8))):
        for d in far:
            kb[field, jnp.where(right_first, 8 - d, 15 + d)] = zeros
    for field, d, halo, first in sent_places():
        kb[field, jnp.where(right_first, 8 - d, 15 + d), pl.ds(16 - halo, 32 + 2 * halo), :] = odd_ref[
            pl.ds(first, 32 + 2 * halo), :
        ]
    for field, both in enumerate((kappas_ref, sources_ref)):
        for i in range(2):
            for p in range(8):
                kb[field, chip_first + 8 * i + p] = both[i, p]

    k, b = kb.at[0], kb.at[1]
    consts = lane_consts(64, 128)

    def first_sweep(p, scaled):
        va[p] = scaled * b[p]

    make_faces(24, k, ax, ay, az, consts, inv, first_sweep)
    sweep(2, 22, va, vb, b, inv, k, ax, ay, az, consts)

    def keep(p, _):
        k0_ref[p] = k[p + 4, pl.ds(8, 48), :]
        b0_ref[p] = b[p + 4, pl.ds(8, 48), :]
        v0_ref[p] = vb[p + 4, pl.ds(8, 48), :]
        inv0_ref[p] = inv[p + 4, pl.ds(8, 48), :]
        return 0

    loop(0, 16, 32, keep, 0)

    def use(p, here, total, _):
        va[p] = b[p] - total
        return 0

    apply_planes(4, 20, vb, k, ax, ay, az, consts, use, 0)

    def coarsen_b(q, _):
        s1[pl.ds((q - 2) * 32, 32), :] = pair_rows(tmp64, va[2 * q] + va[2 * q + 1])
        return 0

    def coarsen_k(q, _):
        sk[pl.ds(q * 32, 32), :] = pair_rows(tmp64, k[2 * q] + k[2 * q + 1])
        return 0

    loop(2, 10, 64, coarsen_b, 0)
    loop(0, 12, 64, coarsen_k, 0)
    b1[pl.ds(2, 8)] = dot(s1[...], pair_matrix(lambda i: i // 2, 0.125)).reshape(8, 32, 128)
    k1_ref[...] = dot(sk[...], pair_matrix(lambda i: i // 2, 0.03125)).reshape(12, 32, 128)

    consts1 = lane_consts(32, 64)
    make_faces(12, k1_ref, ax1, ay1, az1, consts1, inv1_ref)
    va1[pl.ds(2, 8)] = inv1_ref[pl.ds(2, 8)] * b1[pl.ds(2, 8)]
    sweep(3, 9, va1, vb1, b1, inv1_ref, k1_ref, ax1, ay1, az1, consts1)

    def use1(p, here, total, _):
        va1[p] = b1[p] - total
        return 0

    apply_planes(4, 8, vb1, k1_ref, ax1, ay1, az1, consts1, use1, 0)
    for p in range(4):
        vb_ref[p] = vb1[4 + p] + roll(b1[4 + p], 64, 1)

    pay = jnp.zeros((16, 128), F32)
    for part, (field, weight) in enumerate(((va1, 0.125), (k1_ref, 0.03125))):
        for half in range(2):
            place = 64 * part + 32 * half
            rows = pair_rows(tmp32, field[4 + 2 * half] + field[5 + 2 * half])
            pay = pay + dot(rows, pair_matrix(lambda i: jnp.where(i < 64, place + i // 2, -1), weight))
    for i in range(16):
        pay_ref[i] = pay


def middle_kernel(
    all_ref, pay_ref, edge_ref, kw_ref, invw_ref, bw_ref, vw_ref,
    k_ref, inv_ref, b_ref, v_ref, ax, ay, az, va, vb, tmp16, s, sk,
):
    group = iota((16, 128), 1) // 32
    for xl in range(16):
        for part, field in enumerate((b_ref, k_ref)):
            place = 2 * part + xl % 2
            plane = None
            for xh in range(4):
                block = all_ref[(xl // 2) % 2, xl // 4 + 4 * xh]
                moved = block if xh == place else roll(block, 32 * (xh - place), 1)
                plane = moved if plane is None else jnp.where(group == xh, moved, plane)
            field[xl + 1] = plane
    ghosts(k_ref, 18, 32)
    consts = lane_consts(16, 32)
    inv_ref[0] = jnp.zeros((16, 128), F32)
    inv_ref[17] = jnp.zeros((16, 128), F32)
    b_ref[0] = jnp.zeros((16, 128), F32)
    b_ref[17] = jnp.zeros((16, 128), F32)

    def first_sweep(p, scaled):
        va[p] = scaled * b_ref[p]

    make_faces(18, k_ref, ax, ay, az, consts, inv_ref, first_sweep)
    ghosts(va, 18, 32)
    sweep(1, 17, va, v_ref, b_ref, inv_ref, k_ref, ax, ay, az, consts)
    ghosts(v_ref, 18, 32)

    def use(p, here, total, _):
        vb[p] = b_ref[p] - total
        return 0

    apply_planes(1, 17, v_ref, k_ref, ax, ay, az, consts, use, 0)
    sends_b = lax.axis_index("outer") % 2 == 0
    first = 4 * (lax.axis_index("outer") // 2) + 60
    near = []
    for q in range(12):
        x = lax.rem(first + q, 64)
        place = lax.rem(x, 16) + 1
        back = lax.rem(128 - 32 * (x // 16), 128)
        kept = (group == 0) & (first + q >= 64) & (first + q < 128)
        for field, window in ((k_ref, kw_ref), (inv_ref, invw_ref), (b_ref, bw_ref), (v_ref, vw_ref)):
            window[q] = jnp.where(kept, pltpu.roll(field[place], back, 1), 0.0)
        near.append(vw_ref[q] + roll(bw_ref[q], 32, 1))
    for q in range(6):
        both = near[q] + roll(near[q + 6], 64, 1)
        edge_ref[4 * q : 4 * q + 4, :] = jnp.where(sends_b, both[8:12], both[4:8])
    for t in range(8):
        s[t] = pair_rows(tmp16, vb[2 * t + 1] + vb[2 * t + 2])
        sk[t] = pair_rows(tmp16, k_ref[2 * t + 1] + k_ref[2 * t + 2])

    small = jnp.zeros((32, 128), F32)
    for u in range(2):
        m = pair_matrix(lambda i: (i // 32) * 32 + u * 16 + (i % 32) // 2, 0.03125)
        rows = jnp.where(sends_b, 4.0 * s[pl.ds(4 * u, 4)], sk[pl.ds(4 * u, 4)])
        small = small + dot(rows.reshape(32, 128), m)
    for t in range(4):
        vb[0, 4 * t : 4 * t + 4, :] = small[8 * t + 2 : 8 * t + 6, :]
    piece = vb[0]
    for i in range(16):
        pay_ref[i] = piece


def coarse_kernel(
    chip_ref, k2_ref, inv2_ref, b2_ref, v2_ref, odd_ref, k1_ref, inv1_ref,
    k0, b0, v0_ref, inv0, v_out, r_out,
    k3, b3, ax3, ay3, az3, inv3, va3, vb3, c3, tmp16, ax2, ay2, az2, va2, vb2, b2,
    tmp32, b1, va1, vb1, ax1, ay1, az1, tmp64, c1, v0, ax0, ay0, az0, w0,
):
    outer, inner = lax.axis_index("outer"), lax.axis_index("inner")

    for i in range(16):
        for t in range(4):
            b3[t + 1, 4 * i : 4 * i + 4, :] = chip_ref[0, 16 * i + 4 * t : 16 * i + 4 * t + 4, :]
            k3[t + 1, 4 * i : 4 * i + 4, :] = chip_ref[1, 16 * i + 4 * t : 16 * i + 4 * t + 4, :]
    ghosts(k3, 6, 16)
    b3[0] = jnp.zeros((64, 128), F32)
    consts3 = lane_consts(64, 16, True)

    def first_sweep(p, scaled):
        va3[p] = scaled * b3[p]

    make_faces(6, k3, ax3, ay3, az3, consts3, inv3, first_sweep)
    now, later = va3, vb3
    ghosts(now, 6, 16)
    for _ in range(5):
        sweep(1, 5, now, later, b3, inv3, k3, ax3, ay3, az3, consts3)
        now, later = later, now
        ghosts(now, 6, 16)

    def leftover(p, here, total, carry):
        return carry + (b3[p] - total)

    rest = apply_planes(1, 5, now, k3, ax3, ay3, az3, consts3, leftover, jnp.zeros((64, 128), F32))
    lane = iota((64, 128), 1)
    border = jnp.where(lane < 16, 0.5 * k3[1], 0.0) + jnp.where(lane >= 112, 0.5 * k3[4], 0.0)
    for p in range(1, 5):
        border = border + consts3[1] * k3[p]
    shift = jnp.sum(rest, keepdims=True) / jnp.sum(border, keepdims=True)
    for t in range(4):
        c3[t, 0:8, :] = jnp.zeros((8, 128), F32)
        c3[t, 8:72, :] = now[t + 1] + shift
        c3[t, 72:80, :] = jnp.zeros((8, 128), F32)

    near = []
    core = lax.rem(outer, 2)
    for q in range(6):
        x = lax.rem(outer - core + 30 + q, 32)
        back = lax.rem(128 - 16 * (x // 4), 128)
        near.append(pltpu.roll(c3[lax.rem(x, 4), pl.ds(4 * inner + 6, 8), :], back, 1))
    wide = dot(jnp.concatenate(near, axis=0), gather_matrix(lambda j: jnp.where(j < 32, j // 2, -1), 1.0))
    lane = iota((16, 128), 1)
    for q in range(12):
        rows = twice_rows(tmp16, wide[8 * (q // 2) : 8 * (q // 2) + 8])
        below, above = (chip_ref[i, 256 + 4 * (q % 6) : 260 + 4 * (q % 6), :] for i in range(2))
        if q >= 6:
            below, above = roll(below, 64, 1), roll(above, 64, 1)
        v2 = jnp.concatenate([below, v2_ref[q, 4:12, :], above], axis=0)
        b2[q] = jnp.concatenate([roll(below, 96, 1), b2_ref[q, 4:12, :], roll(above, 96, 1)], axis=0)
        va2[q] = jnp.where((lane < 32) & (k2_ref[q] > 0.0), v2 + rows, 0.0)
    consts2 = lane_consts(16, 32)
    make_faces(12, k2_ref, ax2, ay2, az2, consts2)
    sweep(1, 11, va2, vb2, b2, inv2_ref, k2_ref, ax2, ay2, az2, consts2)
    sweep(2, 10, vb2, va2, b2, inv2_ref, k2_ref, ax2, ay2, az2, consts2)

    wide = dot(va2[pl.ds(2 + 2 * core, 6)].reshape(96, 128), gather_matrix(lambda j: jnp.where(j < 64, j // 2, -1), 1.0))
    left_is_odd = outer % 2 == 0
    low = iota((32, 128), 1) < 64
    for q in range(6):
        rows = twice_rows(tmp32, wide[16 * q : 16 * q + 16])
        for p in (2 * q, 2 * q + 1):
            first, second = (chip_ref[i, 280 + 32 * (p % 4) : 312 + 32 * (p % 4), :] for i in range(2))
            if p < 4:
                both = jnp.where(left_is_odd, odd_ref[p], first)
            elif p < 8:
                both = jnp.where(left_is_odd, first, second)
            else:
                both = jnp.where(left_is_odd, second, odd_ref[p - 8])
            b1[p] = roll(both, 64, 1)
            va1[p] = jnp.where(low & (k1_ref[p] > 0.0), both + rows, 0.0)
    consts1 = lane_consts(32, 64)
    make_faces(12, k1_ref, ax1, ay1, az1, consts1)
    sweep(1, 11, va1, vb1, b1, inv1_ref, k1_ref, ax1, ay1, az1, consts1)
    sweep(2, 10, vb1, va1, b1, inv1_ref, k1_ref, ax1, ay1, az1, consts1)

    c1[...] = dot(va1[pl.ds(2, 8)].reshape(256, 128), gather_matrix(lambda j: j // 2, 1.0))

    def correct(q, _):
        twice_rows(tmp64, c1[pl.ds(32 * q, 32), :])
        rows = tmp64[pl.ds(8, 48), :]
        for p in (2 * q, 2 * q + 1):
            v0[p] = jnp.where(k0[p] > 0.0, v0_ref[p] + rows, 0.0)
        return 0

    loop(0, 8, 64, correct, 0)
    consts0 = lane_consts(48, 128)
    make_faces(16, k0, ax0, ay0, az0, consts0)
    sweep(2, 14, v0, w0, b0, inv0, k0, ax0, ay0, az0, consts0)
    sweep(3, 13, w0, v0, b0, inv0, k0, ax0, ay0, az0, consts0)

    def use(p, here, total, _):
        v_out[p - 4] = here[8:40]
        r_out[p - 4] = (b0[p] - total)[8:40]
        return 0

    apply_planes(4, 12, v0, k0, ax0, ay0, az0, consts0, use, 0)


def vmem(*shape):
    return pltpu.VMEM(shape, F32)


def out(*shape):
    return jax.ShapeDtypeStruct(shape, F32)


def call(kernel, name, ins, outs, scratch, args):
    spec = {"v": pl.BlockSpec(memory_space=pltpu.VMEM), "a": pl.BlockSpec(memory_space=pl.ANY)}
    return pl.pallas_call(
        kernel,
        name=name,
        out_shape=outs,
        in_specs=[spec[c] for c in ins],
        out_specs=[spec["v"]] * len(outs),
        scratch_shapes=scratch,
        compiler_params=pltpu.CompilerParams(vmem_limit_bytes=VMEM_LIMIT),
    )(*args)


def body(right_side, codes):
    groups, boxes = lax.axis_size("outer"), lax.axis_size("inner")
    odds = [(i, ((i + 1) ^ 1) - 1) for i in range(1, groups - 1)]
    evens_y = [(i, i ^ 1) for i in range(boxes)]
    odds_y = [(i, ((i + 1) ^ 1) - 1) for i in range(1, boxes - 1)]

    def on_chip(x):
        return lax.all_gather(x, "outer", axis_index_groups=[[i, i + 1] for i in range(0, groups, 2)])

    to_even, to_odd = call(prep_kernel, "prep", "vv", [out(2, 8, 16, 128)] * 2, [], (right_side, codes))
    from_even = lax.ppermute(to_even, "inner", evens_y)
    from_odd = lax.ppermute(to_odd, "inner", odds_y)
    parts = (to_even, to_odd, from_even, from_odd)
    (odd,) = call(pack_kernel, "pack", "vvvv", [out(SENT_ROWS, 128)], [], parts)
    own = call(join_kernel, "join", "vvvva", [out(8, 64, 128)] * 2, [], parts + (odd,))
    odd = lax.ppermute(odd, "outer", odds)
    kappas, sources = (on_chip(x) for x in own)

    fine, level1 = (24, 64, 128), (12, 32, 128)
    pay, vb1, k1, inv1, k0, b0, v0, inv0 = call(
        fine_kernel, "fine", "vvv",
        [out(16, 16, 128), out(4, 32, 128), out(*level1), out(*level1)] + [out(16, 48, 128)] * 4,
        [vmem(2, *fine)] + [vmem(*fine)] * 6 + [vmem(64, 128), vmem(32, 128), vmem(256, 128), vmem(384, 128)]
        + [vmem(*level1)] * 6,
        (kappas, sources, odd),
    )
    same_core = [list(range(c, groups, 2)) for c in range(2)]
    slab = lax.all_to_all(pay, "outer", 0, 0, tiled=True, axis_index_groups=same_core)

    level2, window2 = (18, 16, 128), (12, 16, 128)
    pay3, edge, k2, inv2, b2, v2 = call(
        middle_kernel, "middle", "v",
        [out(16, 16, 128), out(24, 128)] + [out(*window2)] * 4,
        [vmem(*level2)] * 9 + [vmem(16, 128), vmem(8, 8, 128), vmem(8, 8, 128)],
        (on_chip(slab),),
    )
    ups = [(i * boxes + j, i * boxes + j + 1) for i in range(0, groups, 2) for j in range(boxes - 1)]
    downs = [(i * boxes + j + 1, i * boxes + j) for i in range(1, groups, 2) for j in range(boxes - 1)]
    vb1, edge = lax.optimization_barrier((vb1, edge))
    edge = lax.ppermute(edge, ("outer", "inner"), ups + downs)
    odd1 = lax.ppermute(vb1, "outer", odds)
    half = lax.all_to_all(pay3, "inner", 0, 0, tiled=True)
    half, edge, odd1 = lax.optimization_barrier((half, edge, odd1))
    chip = on_chip(jnp.concatenate([half.reshape(256, 128), edge, vb1.reshape(128, 128)], axis=0))

    level3, window = (6, 64, 128), (16, 48, 128)
    return call(
        coarse_kernel, "coarse", "v" * 12,
        [out(8, 32, 128)] * 2,
        [vmem(*level3)] * 8 + [vmem(4, 80, 128), vmem(16, 128)] + [vmem(*window2)] * 6
        + [vmem(32, 128)] + [vmem(*level1)] * 6 + [vmem(64, 128), vmem(256, 128)]
        + [vmem(*window)] * 5,
        (chip, k2, inv2, b2, v2, odd1, k1, inv1, k0, b0, v0, inv0),
    )


def solution(mesh):
    placed = P("outer", "inner", None)
    return jax.shard_map(
        lambda right_side, codes: tuple(body(right_side, codes)),
        mesh=mesh,
        in_specs=(placed, placed),
        out_specs=(placed, placed),
        check_vma=False,
    )
```

```python
import jax
import jax.numpy as jnp
from jax import lax
from jax.experimental import pallas as pl
from jax.experimental.pallas import tpu as pltpu
from jax.sharding import PartitionSpec as P


OMEGA = 0.8
F32 = jnp.float32
VMEM_LIMIT = 24 * 1024 * 1024
UNROLL = 96


def iota(shape, dim):
    return lax.broadcasted_iota(jnp.int32, shape, dim)


def roll(x, shift, axis):
    return pltpu.roll(x, shift % x.shape[axis], axis)


def dot(a, b):
    return jnp.dot(a, b, precision=lax.Precision.HIGHEST, preferred_element_type=F32)


def lane_consts(rows, group, domain_rows=False):
    lane = iota((rows, 128), 1) % group
    zm = jnp.where(lane == group - 1, 0.0, 0.5).astype(F32)
    em = jnp.where((lane == 0) | (lane == group - 1), 0.5, 0.0).astype(F32)
    ym = None
    if domain_rows:
        row = iota((rows, 128), 0)
        ym = jnp.where(row == rows - 1, 0.0, 0.5).astype(F32)
        em = em + jnp.where((row == 0) | (row == rows - 1), 0.5, 0.0).astype(F32)
    return zm, em, ym


def loop(first, last, rows, step, carry):
    count = last - first
    width = max(1, min(count, UNROLL // (rows // 8)))
    whole = count // width

    def block(i, carry):
        for u in range(width):
            carry = step(first + i * width + u, carry)
        return carry

    if whole == 1:
        carry = block(0, carry)
    else:
        carry = lax.fori_loop(0, whole, block, carry)
    for p in range(first + whole * width, last):
        carry = step(p, carry)
    return carry


def make_faces(n, k, ax, ay, az, consts, inv=None, extra=None):
    zm, em, ym = consts

    def step(p, before):
        here = k[p]
        x = 0.5 * (here + k[p + 1])
        y = here + roll(here, -1, 0)
        y = 0.5 * y if ym is None else ym * y
        z = zm * (here + roll(here, -1, 1))
        ax[p] = x
        ay[p] = y
        az[p] = z
        if inv is not None:
            diag = em * here + x + before + y + roll(y, 1, 0) + z + roll(z, 1, 1)
            scaled = jnp.where(here > 0.0, OMEGA / diag, 0.0)
            inv[p] = scaled
            if extra is not None:
                extra(p, scaled)
        return x

    loop(0, n - 1, k.shape[1], step, jnp.zeros(k.shape[1:], F32))


def apply_planes(first, last, v, k, ax, ay, az, consts, use, carry=None):
    em = consts[1]

    def step(p, state):
        before, carry = state
        here = v[p]
        x = ax[p] * (here - v[p + 1])
        y = ay[p] * (here - roll(here, -1, 0))
        z = az[p] * (here - roll(here, -1, 1))
        total = em * k[p] * here + (x - before) + (y - roll(y, 1, 0)) + (z - roll(z, 1, 1))
        return x, use(p, here, total, carry)

    start = ax[first - 1] * (v[first - 1] - v[first])
    return loop(first, last, v.shape[1], step, (start, carry))[1]


def sweep(first, last, v, out, b, inv, k, ax, ay, az, consts):
    def use(p, here, total, _):
        out[p] = here + inv[p] * (b[p] - total)
        return 0

    apply_planes(first, last, v, k, ax, ay, az, consts, use, 0)


def ghosts(ref, n, width):
    lane = iota(ref.shape[1:], 1)
    ref[0] = jnp.where(lane < width, 0.0, roll(ref[n - 2], width, 1))
    ref[n - 1] = jnp.where(lane >= 128 - width, 0.0, roll(ref[1], -width, 1))


def pair_rows(tmp, x):
    half = x.shape[0] // 2
    tmp[...] = x
    return tmp[pl.ds(0, half, 2), :] + tmp[pl.ds(1, half, 2), :]


def twice_rows(tmp, x):
    n = x.shape[0]
    tmp[pl.ds(0, n, 2), :] = x
    tmp[pl.ds(1, n, 2), :] = x
    return tmp[...]


def gather_matrix(source, weight):
    return jnp.where(iota((128, 128), 0) == source(iota((128, 128), 1)), weight, 0.0).astype(F32)


def pair_matrix(target, weight):
    return jnp.where(iota((128, 128), 1) == target(iota((128, 128), 0)), weight, 0.0).astype(F32)


SENT = [(0, d, h) for d, h in zip(range(1, 9), (16, 16, 12, 12, 12, 12, 8, 0))]
SENT += [(1, d, h) for d, h in zip(range(1, 7), (16, 12, 12, 12, 12, 8))]
CORNER_ROWS = sum(2 * h for _, _, h in SENT)


def sent_plane(d):
    return jnp.where(lax.axis_index("outer") % 2 == 1, 8 - d, d - 1)


def prep_kernel(b_ref, codes_ref, even_ref, odd_ref, own_ref, side_ref):
    kappa = jnp.exp(0.5 * codes_ref[...].astype(F32))
    up_first = lax.axis_index("inner") % 2 == 0
    for part, field in enumerate((kappa, b_ref[...])):
        low, high = field[:, :16], field[:, 16:]
        even_ref[part] = jnp.where(up_first, high, low)
        odd_ref[part] = jnp.where(up_first, low, high)
        own_ref[part] = field
    for i, (field, d, _) in enumerate(SENT):
        side_ref[i] = own_ref[field, sent_plane(d)]


def pack_kernel(from_even_ref, from_odd_ref, corner_ref, halo_ref):
    up_first = lax.axis_index("inner") % 2 == 0
    for field in range(2):
        for p in range(8):
            even, odd = from_even_ref[field, p], from_odd_ref[field, p]
            halo_ref[field, p, 0:16, :] = jnp.where(up_first, odd, even)
            halo_ref[field, p, 16:32, :] = jnp.where(up_first, even, odd)
    first = 0
    for field, d, h in SENT:
        if h:
            rows = halo_ref[field, sent_plane(d), 16 - h : 16 + h, :]
            corner_ref[first : first + 2 * h, :] = rows
            first += 2 * h


def fine_kernel(
    chip_ref, halo_ref, side_ref, corner_ref,
    pay_ref, vb_ref, k1_ref, inv1_ref, k0_ref, b0_ref, v0_ref, inv0_ref,
    kb, ax, ay, az, inv, va, vb, tmp64, tmp32, s1, sk, b1, ax1, ay1, az1, va1, vb1,
):
    right_first = lax.axis_index("outer") % 2 == 0
    chip_first = jnp.where(right_first, 8, 0)
    zeros = jnp.zeros((64, 128), F32)
    for field, d in ((1, 7), (1, 8)):
        kb[field, jnp.where(right_first, 8 - d, 15 + d)] = zeros
    first = 0
    for i, (field, d, h) in enumerate(SENT):
        place = jnp.where(right_first, 8 - d, 15 + d)
        if h < 16:
            kb[field, place, 0:16, :] = zeros[0:16]
            kb[field, place, 48:64, :] = zeros[0:16]
        kb[field, place, 16:48, :] = side_ref[i]
        if h:
            kb[field, place, 16 - h : 16, :] = corner_ref[first : first + h, :]
            kb[field, place, 48 : 48 + h, :] = corner_ref[first + h : first + 2 * h, :]
            first += 2 * h
    for field in range(2):
        for i in range(2):
            for p in range(8):
                place = chip_first + 8 * i + p
                kb[field, place, 0:16, :] = halo_ref[i, field, p, 0:16, :]
                kb[field, place, 16:48, :] = chip_ref[i, field, p]
                kb[field, place, 48:64, :] = halo_ref[i, field, p, 16:32, :]

    k, b = kb.at[0], kb.at[1]
    consts = lane_consts(64, 128)

    def first_sweep(p, scaled):
        va[p] = scaled * b[p]

    make_faces(24, k, ax, ay, az, consts, inv, first_sweep)
    sweep(2, 22, va, vb, b, inv, k, ax, ay, az, consts)

    def keep(p, _):
        k0_ref[p] = k[p + 4, pl.ds(8, 48), :]
        b0_ref[p] = b[p + 4, pl.ds(8, 48), :]
        v0_ref[p] = vb[p + 4, pl.ds(8, 48), :]
        inv0_ref[p] = inv[p + 4, pl.ds(8, 48), :]
        return 0

    loop(0, 16, 32, keep, 0)

    def use(p, here, total, _):
        va[p] = b[p] - total
        return 0

    apply_planes(4, 20, vb, k, ax, ay, az, consts, use, 0)

    def coarsen_b(q, _):
        s1[pl.ds((q - 2) * 32, 32), :] = pair_rows(tmp64, va[2 * q] + va[2 * q + 1])
        return 0

    def coarsen_k(q, _):
        sk[pl.ds(q * 32, 32), :] = pair_rows(tmp64, k[2 * q] + k[2 * q + 1])
        return 0

    loop(2, 10, 64, coarsen_b, 0)
    loop(0, 12, 64, coarsen_k, 0)
    b1[pl.ds(2, 8)] = dot(s1[...], pair_matrix(lambda i: i // 2, 0.125)).reshape(8, 32, 128)
    k1_ref[...] = dot(sk[...], pair_matrix(lambda i: i // 2, 0.03125)).reshape(12, 32, 128)

    consts1 = lane_consts(32, 64)
    make_faces(12, k1_ref, ax1, ay1, az1, consts1, inv1_ref)
    va1[pl.ds(2, 8)] = inv1_ref[pl.ds(2, 8)] * b1[pl.ds(2, 8)]
    sweep(3, 9, va1, vb1, b1, inv1_ref, k1_ref, ax1, ay1, az1, consts1)

    def use1(p, here, total, _):
        va1[p] = b1[p] - total
        return 0

    apply_planes(4, 8, vb1, k1_ref, ax1, ay1, az1, consts1, use1, 0)
    for p in range(4):
        vb_ref[p] = vb1[4 + p] + roll(b1[4 + p], 64, 1)

    pay = jnp.zeros((16, 128), F32)
    for part, (field, weight) in enumerate(((va1, 0.125), (k1_ref, 0.03125))):
        for half in range(2):
            place = 64 * part + 32 * half
            rows = pair_rows(tmp32, field[4 + 2 * half] + field[5 + 2 * half])
            pay = pay + dot(rows, pair_matrix(lambda i: jnp.where(i < 64, place + i // 2, -1), weight))
    for i in range(16):
        pay_ref[i] = pay


def middle_kernel(
    all_ref, pay_ref, edge_ref, kw_ref, invw_ref, bw_ref, vw_ref,
    k_ref, inv_ref, b_ref, v_ref, ax, ay, az, va, vb, tmp16, s, sk,
):
    group = iota((16, 128), 1) // 32
    for xl in range(16):
        for part, field in enumerate((b_ref, k_ref)):
            place = 2 * part + xl % 2
            plane = None
            for xh in range(4):
                block = all_ref[(xl // 2) % 2, xl // 4 + 4 * xh]
                moved = block if xh == place else roll(block, 32 * (xh - place), 1)
                plane = moved if plane is None else jnp.where(group == xh, moved, plane)
            field[xl + 1] = plane
    ghosts(k_ref, 18, 32)
    consts = lane_consts(16, 32)
    inv_ref[0] = jnp.zeros((16, 128), F32)
    inv_ref[17] = jnp.zeros((16, 128), F32)
    b_ref[0] = jnp.zeros((16, 128), F32)
    b_ref[17] = jnp.zeros((16, 128), F32)

    def first_sweep(p, scaled):
        va[p] = scaled * b_ref[p]

    make_faces(18, k_ref, ax, ay, az, consts, inv_ref, first_sweep)
    ghosts(va, 18, 32)
    sweep(1, 17, va, v_ref, b_ref, inv_ref, k_ref, ax, ay, az, consts)
    ghosts(v_ref, 18, 32)

    def use(p, here, total, _):
        vb[p] = b_ref[p] - total
        return 0

    apply_planes(1, 17, v_ref, k_ref, ax, ay, az, consts, use, 0)
    sends_b = lax.axis_index("outer") % 2 == 0
    first = 4 * (lax.axis_index("outer") // 2) + 60
    near = []
    for q in range(12):
        x = lax.rem(first + q, 64)
        place = lax.rem(x, 16) + 1
        back = lax.rem(128 - 32 * (x // 16), 128)
        kept = (group == 0) & (first + q >= 64) & (first + q < 128)
        for field, window in ((k_ref, kw_ref), (inv_ref, invw_ref), (b_ref, bw_ref), (v_ref, vw_ref)):
            window[q] = jnp.where(kept, pltpu.roll(field[place], back, 1), 0.0)
        near.append(vw_ref[q] + roll(bw_ref[q], 32, 1))
    for q in range(6):
        both = near[q] + roll(near[q + 6], 64, 1)
        edge_ref[4 * q : 4 * q + 4, :] = jnp.where(sends_b, both[8:12], both[4:8])
    for t in range(8):
        s[t] = pair_rows(tmp16, vb[2 * t + 1] + vb[2 * t + 2])
        sk[t] = pair_rows(tmp16, k_ref[2 * t + 1] + k_ref[2 * t + 2])

    small = jnp.zeros((32, 128), F32)
    for u in range(2):
        m = pair_matrix(lambda i: (i // 32) * 32 + u * 16 + (i % 32) // 2, 0.03125)
        rows = jnp.where(sends_b, 4.0 * s[pl.ds(4 * u, 4)], sk[pl.ds(4 * u, 4)])
        small = small + dot(rows.reshape(32, 128), m)
    for t in range(4):
        vb[0, 4 * t : 4 * t + 4, :] = small[8 * t + 2 : 8 * t + 6, :]
    piece = vb[0]
    for i in range(16):
        pay_ref[i] = piece


def coarse_kernel(
    chip_ref, k2_ref, inv2_ref, b2_ref, v2_ref, odd_ref, k1_ref, inv1_ref,
    k0, b0, v0_ref, inv0, v_out, r_out,
    k3, b3, ax3, ay3, az3, inv3, va3, vb3, c3, tmp16, ax2, ay2, az2, va2, vb2, b2,
    tmp32, b1, va1, vb1, ax1, ay1, az1, tmp64, c1, v0, ax0, ay0, az0, w0,
):
    outer, inner = lax.axis_index("outer"), lax.axis_index("inner")

    for i in range(16):
        for t in range(4):
            b3[t + 1, 4 * i : 4 * i + 4, :] = chip_ref[0, 16 * i + 4 * t : 16 * i + 4 * t + 4, :]
            k3[t + 1, 4 * i : 4 * i + 4, :] = chip_ref[1, 16 * i + 4 * t : 16 * i + 4 * t + 4, :]
    ghosts(k3, 6, 16)
    b3[0] = jnp.zeros((64, 128), F32)
    consts3 = lane_consts(64, 16, True)

    def first_sweep(p, scaled):
        va3[p] = scaled * b3[p]

    make_faces(6, k3, ax3, ay3, az3, consts3, inv3, first_sweep)
    now, later = va3, vb3
    ghosts(now, 6, 16)
    for _ in range(5):
        sweep(1, 5, now, later, b3, inv3, k3, ax3, ay3, az3, consts3)
        now, later = later, now
        ghosts(now, 6, 16)

    def leftover(p, here, total, carry):
        return carry + (b3[p] - total)

    rest = apply_planes(1, 5, now, k3, ax3, ay3, az3, consts3, leftover, jnp.zeros((64, 128), F32))
    lane = iota((64, 128), 1)
    border = jnp.where(lane < 16, 0.5 * k3[1], 0.0) + jnp.where(lane >= 112, 0.5 * k3[4], 0.0)
    for p in range(1, 5):
        border = border + consts3[1] * k3[p]
    shift = jnp.sum(rest, keepdims=True) / jnp.sum(border, keepdims=True)
    for t in range(4):
        c3[t, 0:8, :] = jnp.zeros((8, 128), F32)
        c3[t, 8:72, :] = now[t + 1] + shift
        c3[t, 72:80, :] = jnp.zeros((8, 128), F32)

    near = []
    core = lax.rem(outer, 2)
    for q in range(6):
        x = lax.rem(outer - core + 30 + q, 32)
        back = lax.rem(128 - 16 * (x // 4), 128)
        near.append(pltpu.roll(c3[lax.rem(x, 4), pl.ds(4 * inner + 6, 8), :], back, 1))
    wide = dot(jnp.concatenate(near, axis=0), gather_matrix(lambda j: jnp.where(j < 32, j // 2, -1), 1.0))
    lane = iota((16, 128), 1)
    for q in range(12):
        rows = twice_rows(tmp16, wide[8 * (q // 2) : 8 * (q // 2) + 8])
        below, above = (chip_ref[i, 256 + 4 * (q % 6) : 260 + 4 * (q % 6), :] for i in range(2))
        if q >= 6:
            below, above = roll(below, 64, 1), roll(above, 64, 1)
        v2 = jnp.concatenate([below, v2_ref[q, 4:12, :], above], axis=0)
        b2[q] = jnp.concatenate([roll(below, 96, 1), b2_ref[q, 4:12, :], roll(above, 96, 1)], axis=0)
        va2[q] = jnp.where((lane < 32) & (k2_ref[q] > 0.0), v2 + rows, 0.0)
    consts2 = lane_consts(16, 32)
    make_faces(12, k2_ref, ax2, ay2, az2, consts2)
    sweep(1, 11, va2, vb2, b2, inv2_ref, k2_ref, ax2, ay2, az2, consts2)
    sweep(2, 10, vb2, va2, b2, inv2_ref, k2_ref, ax2, ay2, az2, consts2)

    wide = dot(va2[pl.ds(2 + 2 * core, 6)].reshape(96, 128), gather_matrix(lambda j: jnp.where(j < 64, j // 2, -1), 1.0))
    left_is_odd = outer % 2 == 0
    low = iota((32, 128), 1) < 64
    for q in range(6):
        rows = twice_rows(tmp32, wide[16 * q : 16 * q + 16])
        for p in (2 * q, 2 * q + 1):
            first, second = (chip_ref[i, 280 + 32 * (p % 4) : 312 + 32 * (p % 4), :] for i in range(2))
            if p < 4:
                both = jnp.where(left_is_odd, odd_ref[p], first)
            elif p < 8:
                both = jnp.where(left_is_odd, first, second)
            else:
                both = jnp.where(left_is_odd, second, odd_ref[p - 8])
            b1[p] = roll(both, 64, 1)
            va1[p] = jnp.where(low & (k1_ref[p] > 0.0), both + rows, 0.0)
    consts1 = lane_consts(32, 64)
    make_faces(12, k1_ref, ax1, ay1, az1, consts1)
    sweep(1, 11, va1, vb1, b1, inv1_ref, k1_ref, ax1, ay1, az1, consts1)
    sweep(2, 10, vb1, va1, b1, inv1_ref, k1_ref, ax1, ay1, az1, consts1)

    c1[...] = dot(va1[pl.ds(2, 8)].reshape(256, 128), gather_matrix(lambda j: j // 2, 1.0))

    def correct(q, _):
        twice_rows(tmp64, c1[pl.ds(32 * q, 32), :])
        rows = tmp64[pl.ds(8, 48), :]
        for p in (2 * q, 2 * q + 1):
            v0[p] = jnp.where(k0[p] > 0.0, v0_ref[p] + rows, 0.0)
        return 0

    loop(0, 8, 64, correct, 0)
    consts0 = lane_consts(48, 128)
    make_faces(16, k0, ax0, ay0, az0, consts0)
    sweep(2, 14, v0, w0, b0, inv0, k0, ax0, ay0, az0, consts0)
    sweep(3, 13, w0, v0, b0, inv0, k0, ax0, ay0, az0, consts0)

    def use(p, here, total, _):
        v_out[p - 4] = here[8:40]
        r_out[p - 4] = (b0[p] - total)[8:40]
        return 0

    apply_planes(4, 12, v0, k0, ax0, ay0, az0, consts0, use, 0)


def vmem(*shape):
    return pltpu.VMEM(shape, F32)


def out(*shape):
    return jax.ShapeDtypeStruct(shape, F32)


def call(kernel, name, ins, outs, scratch, args):
    spec = {"v": pl.BlockSpec(memory_space=pltpu.VMEM), "a": pl.BlockSpec(memory_space=pl.ANY)}
    return pl.pallas_call(
        kernel,
        name=name,
        out_shape=outs,
        in_specs=[spec[c] for c in ins],
        out_specs=[spec["v"]] * len(outs),
        scratch_shapes=scratch,
        compiler_params=pltpu.CompilerParams(vmem_limit_bytes=VMEM_LIMIT),
    )(*args)


def body(right_side, codes):
    groups, boxes = lax.axis_size("outer"), lax.axis_size("inner")
    odds = [(i, ((i + 1) ^ 1) - 1) for i in range(1, groups - 1)]
    evens_y = [(i, i ^ 1) for i in range(boxes)]
    odds_y = [(i, ((i + 1) ^ 1) - 1) for i in range(1, boxes - 1)]

    def on_chip(x):
        return lax.all_gather(x, "outer", axis_index_groups=[[i, i + 1] for i in range(0, groups, 2)])

    to_even, to_odd, own, side = call(
        prep_kernel, "prep", "vv",
        [out(2, 8, 16, 128)] * 2 + [out(2, 8, 32, 128), out(len(SENT), 32, 128)], [], (right_side, codes),
    )
    from_even = lax.ppermute(to_even, "inner", evens_y)
    from_odd = lax.ppermute(to_odd, "inner", odds_y)
    side = lax.ppermute(side, "outer", odds)
    chip = on_chip(own)
    corner, halo = call(
        pack_kernel, "pack", "vv", [out(CORNER_ROWS, 128), out(2, 8, 32, 128)], [], (from_even, from_odd)
    )
    corner = lax.ppermute(corner, "outer", odds)
    halo = on_chip(halo)

    fine, level1 = (24, 64, 128), (12, 32, 128)
    pay, vb1, k1, inv1, k0, b0, v0, inv0 = call(
        fine_kernel, "fine", "vvvv",
        [out(16, 16, 128), out(4, 32, 128), out(*level1), out(*level1)] + [out(16, 48, 128)] * 4,
        [vmem(2, *fine)] + [vmem(*fine)] * 6 + [vmem(64, 128), vmem(32, 128), vmem(256, 128), vmem(384, 128)]
        + [vmem(*level1)] * 6,
        (chip, halo, side, corner),
    )
    same_core = [list(range(c, groups, 2)) for c in range(2)]
    slab = lax.all_to_all(pay, "outer", 0, 0, tiled=True, axis_index_groups=same_core)

    level2, window2 = (18, 16, 128), (12, 16, 128)
    pay3, edge, k2, inv2, b2, v2 = call(
        middle_kernel, "middle", "v",
        [out(16, 16, 128), out(24, 128)] + [out(*window2)] * 4,
        [vmem(*level2)] * 9 + [vmem(16, 128), vmem(8, 8, 128), vmem(8, 8, 128)],
        (on_chip(slab),),
    )
    ups = [(i * boxes + j, i * boxes + j + 1) for i in range(0, groups, 2) for j in range(boxes - 1)]
    downs = [(i * boxes + j + 1, i * boxes + j) for i in range(1, groups, 2) for j in range(boxes - 1)]
    vb1, edge = lax.optimization_barrier((vb1, edge))
    odd1 = lax.ppermute(vb1, "outer", odds)
    edge = lax.ppermute(edge, ("outer", "inner"), ups + downs)
    half = lax.all_to_all(pay3, "inner", 0, 0, tiled=True)
    half, edge = lax.optimization_barrier((half, edge))
    chip = on_chip(jnp.concatenate([half.reshape(256, 128), edge, vb1.reshape(128, 128)], axis=0))

    level3, window = (6, 64, 128), (16, 48, 128)
    return call(
        coarse_kernel, "coarse", "v" * 12,
        [out(8, 32, 128)] * 2,
        [vmem(*level3)] * 8 + [vmem(4, 80, 128), vmem(16, 128)] + [vmem(*window2)] * 6
        + [vmem(32, 128)] + [vmem(*level1)] * 6 + [vmem(64, 128), vmem(256, 128)]
        + [vmem(*window)] * 5,
        (chip, k2, inv2, b2, v2, odd1, k1, inv1, k0, b0, v0, inv0),
    )


def solution(mesh):
    placed = P("outer", "inner", None)
    return jax.shard_map(
        lambda right_side, codes: tuple(body(right_side, codes)),
        mesh=mesh,
        in_specs=(placed, placed),
        out_specs=(placed, placed),
        check_vma=False,
    )
```

```python
import jax
import jax.numpy as jnp
from jax import lax
from jax.experimental import pallas as pl
from jax.experimental.pallas import tpu as pltpu
from jax.sharding import PartitionSpec as P


OMEGA = 0.8
F32 = jnp.float32
VMEM_LIMIT = 24 * 1024 * 1024
UNROLL = 96


def iota(shape, dim):
    return lax.broadcasted_iota(jnp.int32, shape, dim)


def roll(x, shift, axis):
    return pltpu.roll(x, shift % x.shape[axis], axis)


def dot(a, b):
    return jnp.dot(a, b, precision=lax.Precision.HIGHEST, preferred_element_type=F32)


def lane_consts(rows, group, domain_rows=False):
    lane = iota((rows, 128), 1) % group
    zm = jnp.where(lane == group - 1, 0.0, 0.5).astype(F32)
    em = jnp.where((lane == 0) | (lane == group - 1), 0.5, 0.0).astype(F32)
    ym = None
    if domain_rows:
        row = iota((rows, 128), 0)
        ym = jnp.where(row == rows - 1, 0.0, 0.5).astype(F32)
        em = em + jnp.where((row == 0) | (row == rows - 1), 0.5, 0.0).astype(F32)
    return zm, em, ym


def loop(first, last, rows, step, carry):
    count = last - first
    width = max(1, min(count, UNROLL // (rows // 8)))
    whole = count // width

    def block(i, carry):
        for u in range(width):
            carry = step(first + i * width + u, carry)
        return carry

    if whole == 1:
        carry = block(0, carry)
    else:
        carry = lax.fori_loop(0, whole, block, carry)
    for p in range(first + whole * width, last):
        carry = step(p, carry)
    return carry


def make_faces(n, k, ax, ay, az, consts, inv=None, extra=None):
    zm, em, ym = consts

    def step(p, before):
        here = k[p]
        x = 0.5 * (here + k[p + 1])
        y = here + roll(here, -1, 0)
        y = 0.5 * y if ym is None else ym * y
        z = zm * (here + roll(here, -1, 1))
        ax[p] = x
        ay[p] = y
        az[p] = z
        if inv is not None:
            diag = em * here + x + before + y + roll(y, 1, 0) + z + roll(z, 1, 1)
            scaled = jnp.where(here > 0.0, OMEGA / diag, 0.0)
            inv[p] = scaled
            if extra is not None:
                extra(p, scaled)
        return x

    loop(0, n - 1, k.shape[1], step, jnp.zeros(k.shape[1:], F32))


def apply_planes(first, last, v, k, ax, ay, az, consts, use, carry=None):
    em = consts[1]

    def step(p, state):
        before, carry = state
        here = v[p]
        x = ax[p] * (here - v[p + 1])
        y = ay[p] * (here - roll(here, -1, 0))
        z = az[p] * (here - roll(here, -1, 1))
        total = em * k[p] * here + (x - before) + (y - roll(y, 1, 0)) + (z - roll(z, 1, 1))
        return x, use(p, here, total, carry)

    start = ax[first - 1] * (v[first - 1] - v[first])
    return loop(first, last, v.shape[1], step, (start, carry))[1]


def sweep(first, last, v, out, b, inv, k, ax, ay, az, consts):
    def use(p, here, total, _):
        out[p] = here + inv[p] * (b[p] - total)
        return 0

    apply_planes(first, last, v, k, ax, ay, az, consts, use, 0)


def ghosts(ref, n, width):
    lane = iota(ref.shape[1:], 1)
    ref[0] = jnp.where(lane < width, 0.0, roll(ref[n - 2], width, 1))
    ref[n - 1] = jnp.where(lane >= 128 - width, 0.0, roll(ref[1], -width, 1))


def pair_rows(tmp, x):
    half = x.shape[0] // 2
    tmp[...] = x
    return tmp[pl.ds(0, half, 2), :] + tmp[pl.ds(1, half, 2), :]


def twice_rows(tmp, x):
    n = x.shape[0]
    tmp[pl.ds(0, n, 2), :] = x
    tmp[pl.ds(1, n, 2), :] = x
    return tmp[...]


def gather_matrix(source, weight):
    return jnp.where(iota((128, 128), 0) == source(iota((128, 128), 1)), weight, 0.0).astype(F32)


def pair_matrix(target, weight):
    return jnp.where(iota((128, 128), 1) == target(iota((128, 128), 0)), weight, 0.0).astype(F32)


SENT = [(0, d, h) for d, h in zip(range(1, 9), (16, 16, 12, 12, 12, 12, 8, 0))]
SENT += [(1, d, h) for d, h in zip(range(1, 7), (16, 12, 12, 12, 12, 8))]
CORNER_ROWS = sum(2 * h for _, _, h in SENT)


def sent_plane(d):
    return jnp.where(lax.axis_index("outer") % 2 == 1, 8 - d, d - 1)


def prep_kernel(b_ref, codes_ref, even_ref, odd_ref, own_ref, side_ref):
    kappa = jnp.exp(0.5 * codes_ref[...].astype(F32))
    up_first = lax.axis_index("inner") % 2 == 0
    for part, field in enumerate((kappa, b_ref[...])):
        low, high = field[:, :16], field[:, 16:]
        even_ref[part] = jnp.where(up_first, high, low)
        odd_ref[part] = jnp.where(up_first, low, high)
        own_ref[part] = field
    for i, (field, d, _) in enumerate(SENT):
        side_ref[i] = own_ref[field, sent_plane(d)]


def pack_kernel(from_even_ref, from_odd_ref, corner_ref, halo_ref):
    up_first = lax.axis_index("inner") % 2 == 0
    for field in range(2):
        for p in range(8):
            even, odd = from_even_ref[field, p], from_odd_ref[field, p]
            halo_ref[field, p, 0:16, :] = jnp.where(up_first, odd, even)
            halo_ref[field, p, 16:32, :] = jnp.where(up_first, even, odd)
    first = 0
    for field, d, h in SENT:
        if h:
            rows = halo_ref[field, sent_plane(d), 16 - h : 16 + h, :]
            corner_ref[first : first + 2 * h, :] = rows
            first += 2 * h


def fine_kernel(
    chip_ref, halo_ref, side_ref, corner_ref,
    pay_ref, vb_ref, k1_ref, inv1_ref, k0_ref, b0_ref, v0_ref, inv0_ref,
    kb, ax, ay, az, inv, va, vb, tmp64, tmp32, s1, sk, b1, ax1, ay1, az1, va1, vb1,
):
    right_first = lax.axis_index("outer") % 2 == 0
    chip_first = jnp.where(right_first, 8, 0)
    zeros = jnp.zeros((64, 128), F32)
    for field, d in ((1, 7), (1, 8)):
        kb[field, jnp.where(right_first, 8 - d, 15 + d)] = zeros
    first = 0
    for i, (field, d, h) in enumerate(SENT):
        place = jnp.where(right_first, 8 - d, 15 + d)
        if h < 16:
            kb[field, place, 0:16, :] = zeros[0:16]
            kb[field, place, 48:64, :] = zeros[0:16]
        kb[field, place, 16:48, :] = side_ref[i]
        if h:
            kb[field, place, 16 - h : 16, :] = corner_ref[first : first + h, :]
            kb[field, place, 48 : 48 + h, :] = corner_ref[first + h : first + 2 * h, :]
            first += 2 * h
    for field in range(2):
        for i in range(2):
            for p in range(8):
                place = chip_first + 8 * i + p
                kb[field, place, 0:16, :] = halo_ref[i, field, p, 0:16, :]
                kb[field, place, 16:48, :] = chip_ref[i, field, p]
                kb[field, place, 48:64, :] = halo_ref[i, field, p, 16:32, :]

    k, b = kb.at[0], kb.at[1]
    consts = lane_consts(64, 128)

    def first_sweep(p, scaled):
        va[p] = scaled * b[p]

    make_faces(24, k, ax, ay, az, consts, inv, first_sweep)
    sweep(2, 22, va, vb, b, inv, k, ax, ay, az, consts)

    def keep(p, _):
        k0_ref[p] = k[p + 4, pl.ds(8, 48), :]
        b0_ref[p] = b[p + 4, pl.ds(8, 48), :]
        v0_ref[p] = vb[p + 4, pl.ds(8, 48), :]
        inv0_ref[p] = inv[p + 4, pl.ds(8, 48), :]
        return 0

    loop(0, 16, 32, keep, 0)

    def use(p, here, total, _):
        va[p] = b[p] - total
        return 0

    apply_planes(4, 20, vb, k, ax, ay, az, consts, use, 0)

    def coarsen_b(q, _):
        s1[pl.ds((q - 2) * 32, 32), :] = pair_rows(tmp64, va[2 * q] + va[2 * q + 1])
        return 0

    def coarsen_k(q, _):
        sk[pl.ds(q * 32, 32), :] = pair_rows(tmp64, k[2 * q] + k[2 * q + 1])
        return 0

    loop(2, 10, 64, coarsen_b, 0)
    loop(0, 12, 64, coarsen_k, 0)
    b1[pl.ds(2, 8)] = dot(s1[...], pair_matrix(lambda i: i // 2, 0.125)).reshape(8, 32, 128)
    k1_ref[...] = dot(sk[...], pair_matrix(lambda i: i // 2, 0.03125)).reshape(12, 32, 128)

    consts1 = lane_consts(32, 64)
    make_faces(12, k1_ref, ax1, ay1, az1, consts1, inv1_ref)
    va1[pl.ds(2, 8)] = inv1_ref[pl.ds(2, 8)] * b1[pl.ds(2, 8)]
    sweep(3, 9, va1, vb1, b1, inv1_ref, k1_ref, ax1, ay1, az1, consts1)

    def use1(p, here, total, _):
        va1[p] = b1[p] - total
        return 0

    apply_planes(4, 8, vb1, k1_ref, ax1, ay1, az1, consts1, use1, 0)
    for p in range(4):
        vb_ref[p] = vb1[4 + p] + roll(b1[4 + p], 64, 1)

    pay = jnp.zeros((16, 128), F32)
    for part, (field, weight) in enumerate(((va1, 0.125), (k1_ref, 0.03125))):
        for half in range(2):
            place = 64 * part + 32 * half
            rows = pair_rows(tmp32, field[4 + 2 * half] + field[5 + 2 * half])
            pay = pay + dot(rows, pair_matrix(lambda i: jnp.where(i < 64, place + i // 2, -1), weight))
    for i in range(32):
        pay_ref[i] = pay


def middle_kernel(
    all_ref, pay_ref, edge_ref, kw_ref, invw_ref, bw_ref, vw_ref,
    k_ref, inv_ref, b_ref, v_ref, ax, ay, az, va, vb, tmp16, s, sk,
):
    group = iota((16, 128), 1) // 32
    for xl in range(16):
        for part, field in enumerate((b_ref, k_ref)):
            place = 2 * part + xl % 2
            plane = None
            for xh in range(4):
                block = all_ref[xl // 2 + 8 * xh]
                moved = block if xh == place else roll(block, 32 * (xh - place), 1)
                plane = moved if plane is None else jnp.where(group == xh, moved, plane)
            field[xl + 1] = plane
    ghosts(k_ref, 18, 32)
    consts = lane_consts(16, 32)
    inv_ref[0] = jnp.zeros((16, 128), F32)
    inv_ref[17] = jnp.zeros((16, 128), F32)
    b_ref[0] = jnp.zeros((16, 128), F32)
    b_ref[17] = jnp.zeros((16, 128), F32)

    def first_sweep(p, scaled):
        va[p] = scaled * b_ref[p]

    make_faces(18, k_ref, ax, ay, az, consts, inv_ref, first_sweep)
    ghosts(va, 18, 32)
    sweep(1, 17, va, v_ref, b_ref, inv_ref, k_ref, ax, ay, az, consts)
    ghosts(v_ref, 18, 32)

    def use(p, here, total, _):
        vb[p] = b_ref[p] - total
        return 0

    apply_planes(1, 17, v_ref, k_ref, ax, ay, az, consts, use, 0)
    sends_b = lax.axis_index("outer") % 2 == 0
    first = 4 * (lax.axis_index("outer") // 2) + 60
    near = []
    for q in range(12):
        x = lax.rem(first + q, 64)
        place = lax.rem(x, 16) + 1
        back = lax.rem(128 - 32 * (x // 16), 128)
        kept = (group == 0) & (first + q >= 64) & (first + q < 128)
        for field, window in ((k_ref, kw_ref), (inv_ref, invw_ref), (b_ref, bw_ref), (v_ref, vw_ref)):
            window[q] = jnp.where(kept, pltpu.roll(field[place], back, 1), 0.0)
        near.append(vw_ref[q] + roll(bw_ref[q], 32, 1))
    for q in range(6):
        both = near[q] + roll(near[q + 6], 64, 1)
        edge_ref[4 * q : 4 * q + 4, :] = jnp.where(sends_b, both[8:12], both[4:8])
    for t in range(8):
        s[t] = pair_rows(tmp16, vb[2 * t + 1] + vb[2 * t + 2])
        sk[t] = pair_rows(tmp16, k_ref[2 * t + 1] + k_ref[2 * t + 2])

    small = jnp.zeros((32, 128), F32)
    for u in range(2):
        m = pair_matrix(lambda i: (i // 32) * 32 + u * 16 + (i % 32) // 2, 0.03125)
        rows = jnp.where(sends_b, 4.0 * s[pl.ds(4 * u, 4)], sk[pl.ds(4 * u, 4)])
        small = small + dot(rows.reshape(32, 128), m)
    for t in range(4):
        vb[0, 4 * t : 4 * t + 4, :] = small[8 * t + 2 : 8 * t + 6, :]
    piece = vb[0]
    for i in range(16):
        pay_ref[i] = piece


def coarse_kernel(
    chip_ref, k2_ref, inv2_ref, b2_ref, v2_ref, odd_ref, k1_ref, inv1_ref,
    k0, b0, v0_ref, inv0, v_out, r_out,
    k3, b3, ax3, ay3, az3, inv3, va3, vb3, c3, tmp16, ax2, ay2, az2, va2, vb2, b2,
    tmp32, b1, va1, vb1, ax1, ay1, az1, tmp64, c1, v0, ax0, ay0, az0, w0,
):
    outer, inner = lax.axis_index("outer"), lax.axis_index("inner")

    for i in range(16):
        for t in range(4):
            b3[t + 1, 4 * i : 4 * i + 4, :] = chip_ref[0, 16 * i + 4 * t : 16 * i + 4 * t + 4, :]
            k3[t + 1, 4 * i : 4 * i + 4, :] = chip_ref[1, 16 * i + 4 * t : 16 * i + 4 * t + 4, :]
    ghosts(k3, 6, 16)
    b3[0] = jnp.zeros((64, 128), F32)
    consts3 = lane_consts(64, 16, True)

    def first_sweep(p, scaled):
        va3[p] = scaled * b3[p]

    make_faces(6, k3, ax3, ay3, az3, consts3, inv3, first_sweep)
    now, later = va3, vb3
    ghosts(now, 6, 16)
    for _ in range(5):
        sweep(1, 5, now, later, b3, inv3, k3, ax3, ay3, az3, consts3)
        now, later = later, now
        ghosts(now, 6, 16)

    def leftover(p, here, total, carry):
        return carry + (b3[p] - total)

    rest = apply_planes(1, 5, now, k3, ax3, ay3, az3, consts3, leftover, jnp.zeros((64, 128), F32))
    lane = iota((64, 128), 1)
    border = jnp.where(lane < 16, 0.5 * k3[1], 0.0) + jnp.where(lane >= 112, 0.5 * k3[4], 0.0)
    for p in range(1, 5):
        border = border + consts3[1] * k3[p]
    shift = jnp.sum(rest, keepdims=True) / jnp.sum(border, keepdims=True)
    for t in range(4):
        c3[t, 0:8, :] = jnp.zeros((8, 128), F32)
        c3[t, 8:72, :] = now[t + 1] + shift
        c3[t, 72:80, :] = jnp.zeros((8, 128), F32)

    near = []
    core = lax.rem(outer, 2)
    for q in range(6):
        x = lax.rem(outer - core + 30 + q, 32)
        back = lax.rem(128 - 16 * (x // 4), 128)
        near.append(pltpu.roll(c3[lax.rem(x, 4), pl.ds(4 * inner + 6, 8), :], back, 1))
    wide = dot(jnp.concatenate(near, axis=0), gather_matrix(lambda j: jnp.where(j < 32, j // 2, -1), 1.0))
    lane = iota((16, 128), 1)
    for q in range(12):
        rows = twice_rows(tmp16, wide[8 * (q // 2) : 8 * (q // 2) + 8])
        below, above = (chip_ref[i, 256 + 4 * (q % 6) : 260 + 4 * (q % 6), :] for i in range(2))
        if q >= 6:
            below, above = roll(below, 64, 1), roll(above, 64, 1)
        v2 = jnp.concatenate([below, v2_ref[q, 4:12, :], above], axis=0)
        b2[q] = jnp.concatenate([roll(below, 96, 1), b2_ref[q, 4:12, :], roll(above, 96, 1)], axis=0)
        va2[q] = jnp.where((lane < 32) & (k2_ref[q] > 0.0), v2 + rows, 0.0)
    consts2 = lane_consts(16, 32)
    make_faces(12, k2_ref, ax2, ay2, az2, consts2)
    sweep(1, 11, va2, vb2, b2, inv2_ref, k2_ref, ax2, ay2, az2, consts2)
    sweep(2, 10, vb2, va2, b2, inv2_ref, k2_ref, ax2, ay2, az2, consts2)

    wide = dot(va2[pl.ds(2 + 2 * core, 6)].reshape(96, 128), gather_matrix(lambda j: jnp.where(j < 64, j // 2, -1), 1.0))
    left_is_odd = outer % 2 == 0
    low = iota((32, 128), 1) < 64
    for q in range(6):
        rows = twice_rows(tmp32, wide[16 * q : 16 * q + 16])
        for p in (2 * q, 2 * q + 1):
            first, second = (chip_ref[i, 280 + 32 * (p % 4) : 312 + 32 * (p % 4), :] for i in range(2))
            if p < 4:
                both = jnp.where(left_is_odd, odd_ref[p], first)
            elif p < 8:
                both = jnp.where(left_is_odd, first, second)
            else:
                both = jnp.where(left_is_odd, second, odd_ref[p - 8])
            b1[p] = roll(both, 64, 1)
            va1[p] = jnp.where(low & (k1_ref[p] > 0.0), both + rows, 0.0)
    consts1 = lane_consts(32, 64)
    make_faces(12, k1_ref, ax1, ay1, az1, consts1)
    sweep(1, 11, va1, vb1, b1, inv1_ref, k1_ref, ax1, ay1, az1, consts1)
    sweep(2, 10, vb1, va1, b1, inv1_ref, k1_ref, ax1, ay1, az1, consts1)

    c1[...] = dot(va1[pl.ds(2, 8)].reshape(256, 128), gather_matrix(lambda j: j // 2, 1.0))

    def correct(q, _):
        twice_rows(tmp64, c1[pl.ds(32 * q, 32), :])
        rows = tmp64[pl.ds(8, 48), :]
        for p in (2 * q, 2 * q + 1):
            v0[p] = jnp.where(k0[p] > 0.0, v0_ref[p] + rows, 0.0)
        return 0

    loop(0, 8, 64, correct, 0)
    consts0 = lane_consts(48, 128)
    make_faces(16, k0, ax0, ay0, az0, consts0)
    sweep(2, 14, v0, w0, b0, inv0, k0, ax0, ay0, az0, consts0)
    sweep(3, 13, w0, v0, b0, inv0, k0, ax0, ay0, az0, consts0)

    def use(p, here, total, _):
        v_out[p - 4] = here[8:40]
        r_out[p - 4] = (b0[p] - total)[8:40]
        return 0

    apply_planes(4, 12, v0, k0, ax0, ay0, az0, consts0, use, 0)


def vmem(*shape):
    return pltpu.VMEM(shape, F32)


def out(*shape):
    return jax.ShapeDtypeStruct(shape, F32)


def call(kernel, name, ins, outs, scratch, args):
    spec = {"v": pl.BlockSpec(memory_space=pltpu.VMEM), "a": pl.BlockSpec(memory_space=pl.ANY)}
    return pl.pallas_call(
        kernel,
        name=name,
        out_shape=outs,
        in_specs=[spec[c] for c in ins],
        out_specs=[spec["v"]] * len(outs),
        scratch_shapes=scratch,
        compiler_params=pltpu.CompilerParams(vmem_limit_bytes=VMEM_LIMIT),
    )(*args)


def body(right_side, codes):
    groups, boxes = lax.axis_size("outer"), lax.axis_size("inner")
    odds = [(i, ((i + 1) ^ 1) - 1) for i in range(1, groups - 1)]
    evens_y = [(i, i ^ 1) for i in range(boxes)]
    odds_y = [(i, ((i + 1) ^ 1) - 1) for i in range(1, boxes - 1)]

    def on_chip(x):
        return lax.all_gather(x, "outer", axis_index_groups=[[i, i + 1] for i in range(0, groups, 2)])

    to_even, to_odd, own, side = call(
        prep_kernel, "prep", "vv",
        [out(2, 8, 16, 128)] * 2 + [out(2, 8, 32, 128), out(len(SENT), 32, 128)], [], (right_side, codes),
    )
    from_even = lax.ppermute(to_even, "inner", evens_y)
    from_odd = lax.ppermute(to_odd, "inner", odds_y)
    side = lax.ppermute(side, "outer", odds)
    chip = on_chip(own)
    corner, halo = call(
        pack_kernel, "pack", "vv", [out(CORNER_ROWS, 128), out(2, 8, 32, 128)], [], (from_even, from_odd)
    )
    corner = lax.ppermute(corner, "outer", odds)
    halo = on_chip(halo)

    fine, level1 = (24, 64, 128), (12, 32, 128)
    pay, vb1, k1, inv1, k0, b0, v0, inv0 = call(
        fine_kernel, "fine", "vvvv",
        [out(32, 16, 128), out(4, 32, 128), out(*level1), out(*level1)] + [out(16, 48, 128)] * 4,
        [vmem(2, *fine)] + [vmem(*fine)] * 6 + [vmem(64, 128), vmem(32, 128), vmem(256, 128), vmem(384, 128)]
        + [vmem(*level1)] * 6,
        (chip, halo, side, corner),
    )
    slab = lax.all_to_all(pay, "outer", 0, 0, tiled=True)

    level2, window2 = (18, 16, 128), (12, 16, 128)
    pay3, edge, k2, inv2, b2, v2 = call(
        middle_kernel, "middle", "v",
        [out(16, 16, 128), out(24, 128)] + [out(*window2)] * 4,
        [vmem(*level2)] * 9 + [vmem(16, 128), vmem(8, 8, 128), vmem(8, 8, 128)],
        (slab,),
    )
    ups = [(i * boxes + j, i * boxes + j + 1) for i in range(0, groups, 2) for j in range(boxes - 1)]
    downs = [(i * boxes + j + 1, i * boxes + j) for i in range(1, groups, 2) for j in range(boxes - 1)]
    vb1, edge = lax.optimization_barrier((vb1, edge))
    odd1 = lax.ppermute(vb1, "outer", odds)
    edge = lax.ppermute(edge, ("outer", "inner"), ups + downs)
    half = lax.all_to_all(pay3, "inner", 0, 0, tiled=True)
    half, edge = lax.optimization_barrier((half, edge))
    chip = on_chip(jnp.concatenate([half.reshape(256, 128), edge, vb1.reshape(128, 128)], axis=0))

    level3, window = (6, 64, 128), (16, 48, 128)
    return call(
        coarse_kernel, "coarse", "v" * 12,
        [out(8, 32, 128)] * 2,
        [vmem(*level3)] * 8 + [vmem(4, 80, 128), vmem(16, 128)] + [vmem(*window2)] * 6
        + [vmem(32, 128)] + [vmem(*level1)] * 6 + [vmem(64, 128), vmem(256, 128)]
        + [vmem(*window)] * 5,
        (chip, k2, inv2, b2, v2, odd1, k1, inv1, k0, b0, v0, inv0),
    )


def solution(mesh):
    placed = P("outer", "inner", None)
    return jax.shard_map(
        lambda right_side, codes: tuple(body(right_side, codes)),
        mesh=mesh,
        in_specs=(placed, placed),
        out_specs=(placed, placed),
        check_vma=False,
    )
```

```python
import jax
import jax.numpy as jnp
from jax import lax
from jax.experimental import pallas as pl
from jax.experimental.pallas import tpu as pltpu
from jax.sharding import PartitionSpec as P


OMEGA = 0.8
F32 = jnp.float32
VMEM_LIMIT = 24 * 1024 * 1024
UNROLL = 96


def iota(shape, dim):
    return lax.broadcasted_iota(jnp.int32, shape, dim)


def roll(x, shift, axis):
    return pltpu.roll(x, shift % x.shape[axis], axis)


def dot(a, b):
    return jnp.dot(a, b, precision=lax.Precision.HIGHEST, preferred_element_type=F32)


def lane_consts(rows, group, domain_rows=False):
    lane = iota((rows, 128), 1) % group
    zm = jnp.where(lane == group - 1, 0.0, 0.5).astype(F32)
    em = jnp.where((lane == 0) | (lane == group - 1), 0.5, 0.0).astype(F32)
    ym = None
    if domain_rows:
        row = iota((rows, 128), 0)
        ym = jnp.where(row == rows - 1, 0.0, 0.5).astype(F32)
        em = em + jnp.where((row == 0) | (row == rows - 1), 0.5, 0.0).astype(F32)
    return zm, em, ym


def loop(first, last, rows, step, carry):
    count = last - first
    width = max(1, min(count, UNROLL // (rows // 8)))
    whole = count // width

    def block(i, carry):
        for u in range(width):
            carry = step(first + i * width + u, carry)
        return carry

    if whole == 1:
        carry = block(0, carry)
    else:
        carry = lax.fori_loop(0, whole, block, carry)
    for p in range(first + whole * width, last):
        carry = step(p, carry)
    return carry


def make_faces(n, k, ax, ay, az, consts, inv=None, extra=None):
    zm, em, ym = consts

    def step(p, before):
        here = k[p]
        x = 0.5 * (here + k[p + 1])
        y = here + roll(here, -1, 0)
        y = 0.5 * y if ym is None else ym * y
        z = zm * (here + roll(here, -1, 1))
        ax[p] = x
        ay[p] = y
        az[p] = z
        if inv is not None:
            diag = em * here + x + before + y + roll(y, 1, 0) + z + roll(z, 1, 1)
            scaled = jnp.where(here > 0.0, OMEGA / diag, 0.0)
            inv[p] = scaled
            if extra is not None:
                extra(p, scaled)
        return x

    loop(0, n - 1, k.shape[1], step, jnp.zeros(k.shape[1:], F32))


def apply_planes(first, last, v, k, ax, ay, az, consts, use, carry=None):
    em = consts[1]

    def step(p, state):
        before, carry = state
        here = v[p]
        x = ax[p] * (here - v[p + 1])
        y = ay[p] * (here - roll(here, -1, 0))
        z = az[p] * (here - roll(here, -1, 1))
        total = em * k[p] * here + (x - before) + (y - roll(y, 1, 0)) + (z - roll(z, 1, 1))
        return x, use(p, here, total, carry)

    start = ax[first - 1] * (v[first - 1] - v[first])
    return loop(first, last, v.shape[1], step, (start, carry))[1]


def sweep(first, last, v, out, b, inv, k, ax, ay, az, consts):
    def use(p, here, total, _):
        out[p] = here + inv[p] * (b[p] - total)
        return 0

    apply_planes(first, last, v, k, ax, ay, az, consts, use, 0)


def ghosts(ref, n, width):
    lane = iota(ref.shape[1:], 1)
    ref[0] = jnp.where(lane < width, 0.0, roll(ref[n - 2], width, 1))
    ref[n - 1] = jnp.where(lane >= 128 - width, 0.0, roll(ref[1], -width, 1))


def pair_rows(tmp, x):
    half = x.shape[0] // 2
    tmp[...] = x
    return tmp[pl.ds(0, half, 2), :] + tmp[pl.ds(1, half, 2), :]


def twice_rows(tmp, x):
    n = x.shape[0]
    tmp[pl.ds(0, n, 2), :] = x
    tmp[pl.ds(1, n, 2), :] = x
    return tmp[...]


def gather_matrix(source, weight):
    return jnp.where(iota((128, 128), 0) == source(iota((128, 128), 1)), weight, 0.0).astype(F32)


def pair_matrix(target, weight):
    return jnp.where(iota((128, 128), 1) == target(iota((128, 128), 0)), weight, 0.0).astype(F32)


SENT = [(0, d, h) for d, h in zip(range(1, 9), (16, 16, 12, 12, 12, 12, 8, 0))]
SENT += [(1, d, h) for d, h in zip(range(1, 7), (16, 12, 12, 12, 12, 8))]
CORNER_ROWS = sum(2 * h for _, _, h in SENT)


def sent_plane(d, on_chip):
    return jnp.where(lax.axis_index("outer") % 2 == (0 if on_chip else 1), 8 - d, d - 1)


def prep_kernel(b_ref, codes_ref, even_ref, odd_ref, own_ref, side_ref):
    kappa = jnp.exp(0.5 * codes_ref[...].astype(F32))
    up_first = lax.axis_index("inner") % 2 == 0
    for part, field in enumerate((kappa, b_ref[...])):
        low, high = field[:, :16], field[:, 16:]
        even_ref[part] = jnp.where(up_first, high, low)
        odd_ref[part] = jnp.where(up_first, low, high)
        own_ref[part] = field
    for i, (field, d, _) in enumerate(SENT):
        side_ref[i] = own_ref[field, sent_plane(d, False)]


def pack_kernel(from_even_ref, from_odd_ref, own_ref, corner_ref, halo_ref, chip_ref):
    up_first = lax.axis_index("inner") % 2 == 0
    for field in range(2):
        for p in range(8):
            even, odd = from_even_ref[field, p], from_odd_ref[field, p]
            halo_ref[field, p, 0:16, :] = jnp.where(up_first, odd, even)
            halo_ref[field, p, 16:32, :] = jnp.where(up_first, even, odd)
    first = 0
    for i, (field, d, h) in enumerate(SENT):
        chip_ref[32 * i : 32 * i + 32, :] = own_ref[field, sent_plane(d, True)]
        if h:
            corner_ref[first : first + 2 * h, :] = halo_ref[field, sent_plane(d, False), 16 - h : 16 + h, :]
            place = 32 * len(SENT) + first
            chip_ref[place : place + 2 * h, :] = halo_ref[field, sent_plane(d, True), 16 - h : 16 + h, :]
            first += 2 * h


def fine_kernel(
    own_ref, halo_ref, chip_ref, side_ref, corner_ref,
    pay_ref, vb_ref, k1_ref, inv1_ref, k0_ref, b0_ref, v0_ref, inv0_ref,
    kb, ax, ay, az, inv, va, vb, tmp64, tmp32, s1, sk, b1, ax1, ay1, az1, va1, vb1,
):
    core = lax.axis_index("outer") % 2
    zeros = jnp.zeros((64, 128), F32)
    for place in (0, 1, 22, 23):
        kb[1, place] = zeros
    first = 0
    for i, (field, d, h) in enumerate(SENT):
        for on_chip in (False, True):
            place = jnp.where(core == (1 if on_chip else 0), 8 - d, 15 + d)
            if h < 16:
                kb[field, place, 0:16, :] = zeros[0:16]
                kb[field, place, 48:64, :] = zeros[0:16]
            kb[field, place, 16:48, :] = chip_ref[1 - core, 32 * i : 32 * i + 32, :] if on_chip else side_ref[i]
            if h:
                corners, start = (chip_ref.at[1 - core], 32 * len(SENT) + first) if on_chip else (corner_ref, first)
                kb[field, place, 16 - h : 16, :] = corners[start : start + h, :]
                kb[field, place, 48 : 48 + h, :] = corners[start + h : start + 2 * h, :]
        first += 2 * h
    for field in range(2):
        for p in range(8):
            kb[field, 8 + p, 0:16, :] = halo_ref[field, p, 0:16, :]
            kb[field, 8 + p, 16:48, :] = own_ref[field, p]
            kb[field, 8 + p, 48:64, :] = halo_ref[field, p, 16:32, :]

    k, b = kb.at[0], kb.at[1]
    consts = lane_consts(64, 128)

    def first_sweep(p, scaled):
        va[p] = scaled * b[p]

    make_faces(24, k, ax, ay, az, consts, inv, first_sweep)
    sweep(2, 22, va, vb, b, inv, k, ax, ay, az, consts)

    def keep(p, _):
        k0_ref[p] = k[p + 4, pl.ds(8, 48), :]
        b0_ref[p] = b[p + 4, pl.ds(8, 48), :]
        v0_ref[p] = vb[p + 4, pl.ds(8, 48), :]
        inv0_ref[p] = inv[p + 4, pl.ds(8, 48), :]
        return 0

    loop(0, 16, 32, keep, 0)

    def use(p, here, total, _):
        va[p] = b[p] - total
        return 0

    apply_planes(4, 20, vb, k, ax, ay, az, consts, use, 0)

    def coarsen_b(q, _):
        s1[pl.ds((q - 2) * 32, 32), :] = pair_rows(tmp64, va[2 * q] + va[2 * q + 1])
        return 0

    def coarsen_k(q, _):
        sk[pl.ds(q * 32, 32), :] = pair_rows(tmp64, k[2 * q] + k[2 * q + 1])
        return 0

    loop(2, 10, 64, coarsen_b, 0)
    loop(0, 12, 64, coarsen_k, 0)
    b1[pl.ds(2, 8)] = dot(s1[...], pair_matrix(lambda i: i // 2, 0.125)).reshape(8, 32, 128)
    k1_ref[...] = dot(sk[...], pair_matrix(lambda i: i // 2, 0.03125)).reshape(12, 32, 128)

    consts1 = lane_consts(32, 64)
    make_faces(12, k1_ref, ax1, ay1, az1, consts1, inv1_ref)
    va1[pl.ds(2, 8)] = inv1_ref[pl.ds(2, 8)] * b1[pl.ds(2, 8)]
    sweep(3, 9, va1, vb1, b1, inv1_ref, k1_ref, ax1, ay1, az1, consts1)

    def use1(p, here, total, _):
        va1[p] = b1[p] - total
        return 0

    apply_planes(4, 8, vb1, k1_ref, ax1, ay1, az1, consts1, use1, 0)
    for p in range(4):
        vb_ref[p] = vb1[4 + p] + roll(b1[4 + p], 64, 1)

    pay = jnp.zeros((16, 128), F32)
    for part, (field, weight) in enumerate(((va1, 0.125), (k1_ref, 0.03125))):
        for half in range(2):
            place = 64 * part + 32 * half
            rows = pair_rows(tmp32, field[4 + 2 * half] + field[5 + 2 * half])
            pay = pay + dot(rows, pair_matrix(lambda i: jnp.where(i < 64, place + i // 2, -1), weight))
    for i in range(32):
        pay_ref[i] = pay


def middle_kernel(
    all_ref, pay_ref, edge_ref, kw_ref, invw_ref, bw_ref, vw_ref,
    k_ref, inv_ref, b_ref, v_ref, ax, ay, az, va, vb, tmp16, s, sk,
):
    group = iota((16, 128), 1) // 32
    for xl in range(16):
        for part, field in enumerate((b_ref, k_ref)):
            place = 2 * part + xl % 2
            plane = None
            for xh in range(4):
                block = all_ref[xl // 2 + 8 * xh]
                moved = block if xh == place else roll(block, 32 * (xh - place), 1)
                plane = moved if plane is None else jnp.where(group == xh, moved, plane)
            field[xl + 1] = plane
    ghosts(k_ref, 18, 32)
    consts = lane_consts(16, 32)
    inv_ref[0] = jnp.zeros((16, 128), F32)
    inv_ref[17] = jnp.zeros((16, 128), F32)
    b_ref[0] = jnp.zeros((16, 128), F32)
    b_ref[17] = jnp.zeros((16, 128), F32)

    def first_sweep(p, scaled):
        va[p] = scaled * b_ref[p]

    make_faces(18, k_ref, ax, ay, az, consts, inv_ref, first_sweep)
    ghosts(va, 18, 32)
    sweep(1, 17, va, v_ref, b_ref, inv_ref, k_ref, ax, ay, az, consts)
    ghosts(v_ref, 18, 32)

    def use(p, here, total, _):
        vb[p] = b_ref[p] - total
        return 0

    apply_planes(1, 17, v_ref, k_ref, ax, ay, az, consts, use, 0)
    sends_b = lax.axis_index("outer") % 2 == 0
    first = 4 * (lax.axis_index("outer") // 2) + 60
    near = []
    for q in range(12):
        x = lax.rem(first + q, 64)
        place = lax.rem(x, 16) + 1
        back = lax.rem(128 - 32 * (x // 16), 128)
        kept = (group == 0) & (first + q >= 64) & (first + q < 128)
        for field, window in ((k_ref, kw_ref), (inv_ref, invw_ref), (b_ref, bw_ref), (v_ref, vw_ref)):
            window[q] = jnp.where(kept, pltpu.roll(field[place], back, 1), 0.0)
        near.append(vw_ref[q] + roll(bw_ref[q], 32, 1))
    for q in range(6):
        both = near[q] + roll(near[q + 6], 64, 1)
        edge_ref[4 * q : 4 * q + 4, :] = jnp.where(sends_b, both[8:12], both[4:8])
    for t in range(8):
        s[t] = pair_rows(tmp16, vb[2 * t + 1] + vb[2 * t + 2])
        sk[t] = pair_rows(tmp16, k_ref[2 * t + 1] + k_ref[2 * t + 2])

    small = jnp.zeros((32, 128), F32)
    for u in range(2):
        m = pair_matrix(lambda i: (i // 32) * 32 + u * 16 + (i % 32) // 2, 0.03125)
        rows = jnp.where(sends_b, 4.0 * s[pl.ds(4 * u, 4)], sk[pl.ds(4 * u, 4)])
        small = small + dot(rows.reshape(32, 128), m)
    for t in range(4):
        vb[0, 4 * t : 4 * t + 4, :] = small[8 * t + 2 : 8 * t + 6, :]
    piece = vb[0]
    for i in range(16):
        pay_ref[i] = piece


def coarse_kernel(
    chip_ref, k2_ref, inv2_ref, b2_ref, v2_ref, odd_ref, k1_ref, inv1_ref,
    k0, b0, v0_ref, inv0, v_out, r_out,
    k3, b3, ax3, ay3, az3, inv3, va3, vb3, c3, tmp16, ax2, ay2, az2, va2, vb2, b2,
    tmp32, b1, va1, vb1, ax1, ay1, az1, tmp64, c1, v0, ax0, ay0, az0, w0,
):
    outer, inner = lax.axis_index("outer"), lax.axis_index("inner")

    for i in range(16):
        for t in range(4):
            b3[t + 1, 4 * i : 4 * i + 4, :] = chip_ref[0, 16 * i + 4 * t : 16 * i + 4 * t + 4, :]
            k3[t + 1, 4 * i : 4 * i + 4, :] = chip_ref[1, 16 * i + 4 * t : 16 * i + 4 * t + 4, :]
    ghosts(k3, 6, 16)
    b3[0] = jnp.zeros((64, 128), F32)
    consts3 = lane_consts(64, 16, True)

    def first_sweep(p, scaled):
        va3[p] = scaled * b3[p]

    make_faces(6, k3, ax3, ay3, az3, consts3, inv3, first_sweep)
    now, later = va3, vb3
    ghosts(now, 6, 16)
    for _ in range(5):
        sweep(1, 5, now, later, b3, inv3, k3, ax3, ay3, az3, consts3)
        now, later = later, now
        ghosts(now, 6, 16)

    def leftover(p, here, total, carry):
        return carry + (b3[p] - total)

    rest = apply_planes(1, 5, now, k3, ax3, ay3, az3, consts3, leftover, jnp.zeros((64, 128), F32))
    lane = iota((64, 128), 1)
    border = jnp.where(lane < 16, 0.5 * k3[1], 0.0) + jnp.where(lane >= 112, 0.5 * k3[4], 0.0)
    for p in range(1, 5):
        border = border + consts3[1] * k3[p]
    shift = jnp.sum(rest, keepdims=True) / jnp.sum(border, keepdims=True)
    for t in range(4):
        c3[t, 0:8, :] = jnp.zeros((8, 128), F32)
        c3[t, 8:72, :] = now[t + 1] + shift
        c3[t, 72:80, :] = jnp.zeros((8, 128), F32)

    near = []
    core = lax.rem(outer, 2)
    for q in range(6):
        x = lax.rem(outer - core + 30 + q, 32)
        back = lax.rem(128 - 16 * (x // 4), 128)
        near.append(pltpu.roll(c3[lax.rem(x, 4), pl.ds(4 * inner + 6, 8), :], back, 1))
    wide = dot(jnp.concatenate(near, axis=0), gather_matrix(lambda j: jnp.where(j < 32, j // 2, -1), 1.0))
    lane = iota((16, 128), 1)
    for q in range(12):
        rows = twice_rows(tmp16, wide[8 * (q // 2) : 8 * (q // 2) + 8])
        below, above = (chip_ref[i, 256 + 4 * (q % 6) : 260 + 4 * (q % 6), :] for i in range(2))
        if q >= 6:
            below, above = roll(below, 64, 1), roll(above, 64, 1)
        v2 = jnp.concatenate([below, v2_ref[q, 4:12, :], above], axis=0)
        b2[q] = jnp.concatenate([roll(below, 96, 1), b2_ref[q, 4:12, :], roll(above, 96, 1)], axis=0)
        va2[q] = jnp.where((lane < 32) & (k2_ref[q] > 0.0), v2 + rows, 0.0)
    consts2 = lane_consts(16, 32)
    make_faces(12, k2_ref, ax2, ay2, az2, consts2)
    sweep(1, 11, va2, vb2, b2, inv2_ref, k2_ref, ax2, ay2, az2, consts2)
    sweep(2, 10, vb2, va2, b2, inv2_ref, k2_ref, ax2, ay2, az2, consts2)

    wide = dot(va2[pl.ds(2 + 2 * core, 6)].reshape(96, 128), gather_matrix(lambda j: jnp.where(j < 64, j // 2, -1), 1.0))
    left_is_odd = outer % 2 == 0
    low = iota((32, 128), 1) < 64
    for q in range(6):
        rows = twice_rows(tmp32, wide[16 * q : 16 * q + 16])
        for p in (2 * q, 2 * q + 1):
            first, second = (chip_ref[i, 280 + 32 * (p % 4) : 312 + 32 * (p % 4), :] for i in range(2))
            if p < 4:
                both = jnp.where(left_is_odd, odd_ref[p], first)
            elif p < 8:
                both = jnp.where(left_is_odd, first, second)
            else:
                both = jnp.where(left_is_odd, second, odd_ref[p - 8])
            b1[p] = roll(both, 64, 1)
            va1[p] = jnp.where(low & (k1_ref[p] > 0.0), both + rows, 0.0)
    consts1 = lane_consts(32, 64)
    make_faces(12, k1_ref, ax1, ay1, az1, consts1)
    sweep(1, 11, va1, vb1, b1, inv1_ref, k1_ref, ax1, ay1, az1, consts1)
    sweep(2, 10, vb1, va1, b1, inv1_ref, k1_ref, ax1, ay1, az1, consts1)

    c1[...] = dot(va1[pl.ds(2, 8)].reshape(256, 128), gather_matrix(lambda j: j // 2, 1.0))

    def correct(q, _):
        twice_rows(tmp64, c1[pl.ds(32 * q, 32), :])
        rows = tmp64[pl.ds(8, 48), :]
        for p in (2 * q, 2 * q + 1):
            v0[p] = jnp.where(k0[p] > 0.0, v0_ref[p] + rows, 0.0)
        return 0

    loop(0, 8, 64, correct, 0)
    consts0 = lane_consts(48, 128)
    make_faces(16, k0, ax0, ay0, az0, consts0)
    sweep(2, 14, v0, w0, b0, inv0, k0, ax0, ay0, az0, consts0)
    sweep(3, 13, w0, v0, b0, inv0, k0, ax0, ay0, az0, consts0)

    def use(p, here, total, _):
        v_out[p - 4] = here[8:40]
        r_out[p - 4] = (b0[p] - total)[8:40]
        return 0

    apply_planes(4, 12, v0, k0, ax0, ay0, az0, consts0, use, 0)


def vmem(*shape):
    return pltpu.VMEM(shape, F32)


def out(*shape):
    return jax.ShapeDtypeStruct(shape, F32)


def call(kernel, name, ins, outs, scratch, args):
    spec = {"v": pl.BlockSpec(memory_space=pltpu.VMEM), "a": pl.BlockSpec(memory_space=pl.ANY)}
    return pl.pallas_call(
        kernel,
        name=name,
        out_shape=outs,
        in_specs=[spec[c] for c in ins],
        out_specs=[spec["v"]] * len(outs),
        scratch_shapes=scratch,
        compiler_params=pltpu.CompilerParams(vmem_limit_bytes=VMEM_LIMIT),
    )(*args)


def body(right_side, codes):
    groups, boxes = lax.axis_size("outer"), lax.axis_size("inner")
    odds = [(i, ((i + 1) ^ 1) - 1) for i in range(1, groups - 1)]
    evens_y = [(i, i ^ 1) for i in range(boxes)]
    odds_y = [(i, ((i + 1) ^ 1) - 1) for i in range(1, boxes - 1)]

    def on_chip(x):
        return lax.all_gather(x, "outer", axis_index_groups=[[i, i + 1] for i in range(0, groups, 2)])

    to_even, to_odd, own, side = call(
        prep_kernel, "prep", "vv",
        [out(2, 8, 16, 128)] * 2 + [out(2, 8, 32, 128), out(len(SENT), 32, 128)], [], (right_side, codes),
    )
    from_even = lax.ppermute(to_even, "inner", evens_y)
    from_odd = lax.ppermute(to_odd, "inner", odds_y)
    side = lax.ppermute(side, "outer", odds)
    corner, halo, chip = call(
        pack_kernel, "pack", "vvv",
        [out(CORNER_ROWS, 128), out(2, 8, 32, 128), out(32 * len(SENT) + CORNER_ROWS, 128)], [],
        (from_even, from_odd, own),
    )
    corner = lax.ppermute(corner, "outer", odds)
    chip = on_chip(chip)

    fine, level1 = (24, 64, 128), (12, 32, 128)
    pay, vb1, k1, inv1, k0, b0, v0, inv0 = call(
        fine_kernel, "fine", "vvvvv",
        [out(32, 16, 128), out(4, 32, 128), out(*level1), out(*level1)] + [out(16, 48, 128)] * 4,
        [vmem(2, *fine)] + [vmem(*fine)] * 6 + [vmem(64, 128), vmem(32, 128), vmem(256, 128), vmem(384, 128)]
        + [vmem(*level1)] * 6,
        (own, halo, chip, side, corner),
    )
    slab = lax.all_to_all(pay, "outer", 0, 0, tiled=True)

    level2, window2 = (18, 16, 128), (12, 16, 128)
    pay3, edge, k2, inv2, b2, v2 = call(
        middle_kernel, "middle", "v",
        [out(16, 16, 128), out(24, 128)] + [out(*window2)] * 4,
        [vmem(*level2)] * 9 + [vmem(16, 128), vmem(8, 8, 128), vmem(8, 8, 128)],
        (slab,),
    )
    ups = [(i * boxes + j, i * boxes + j + 1) for i in range(0, groups, 2) for j in range(boxes - 1)]
    downs = [(i * boxes + j + 1, i * boxes + j) for i in range(1, groups, 2) for j in range(boxes - 1)]
    vb1, edge = lax.optimization_barrier((vb1, edge))
    odd1 = lax.ppermute(vb1, "outer", odds)
    edge = lax.ppermute(edge, ("outer", "inner"), ups + downs)
    half = lax.all_to_all(pay3, "inner", 0, 0, tiled=True)
    half, edge = lax.optimization_barrier((half, edge))
    chip = on_chip(jnp.concatenate([half.reshape(256, 128), edge, vb1.reshape(128, 128)], axis=0))

    level3, window = (6, 64, 128), (16, 48, 128)
    return call(
        coarse_kernel, "coarse", "v" * 12,
        [out(8, 32, 128)] * 2,
        [vmem(*level3)] * 8 + [vmem(4, 80, 128), vmem(16, 128)] + [vmem(*window2)] * 6
        + [vmem(32, 128)] + [vmem(*level1)] * 6 + [vmem(64, 128), vmem(256, 128)]
        + [vmem(*window)] * 5,
        (chip, k2, inv2, b2, v2, odd1, k1, inv1, k0, b0, v0, inv0),
    )


def solution(mesh):
    placed = P("outer", "inner", None)
    return jax.shard_map(
        lambda right_side, codes: tuple(body(right_side, codes)),
        mesh=mesh,
        in_specs=(placed, placed),
        out_specs=(placed, placed),
        check_vma=False,
    )
```

```python
import jax
import jax.numpy as jnp
from jax import lax
from jax.experimental import pallas as pl
from jax.experimental.pallas import tpu as pltpu
from jax.sharding import PartitionSpec as P


OMEGA = 0.8
F32 = jnp.float32
VMEM_LIMIT = 24 * 1024 * 1024
UNROLL = 96


def iota(shape, dim):
    return lax.broadcasted_iota(jnp.int32, shape, dim)


def roll(x, shift, axis):
    return pltpu.roll(x, shift % x.shape[axis], axis)


def dot(a, b):
    b = b.astype(jnp.bfloat16)
    total = None
    for _ in range(3):
        part = a.astype(jnp.bfloat16)
        a = a - part.astype(F32)
        product = jnp.dot(part, b, preferred_element_type=F32)
        total = product if total is None else total + product
    return total


def lane_consts(rows, group, domain_rows=False):
    lane = iota((rows, 128), 1) % group
    zm = jnp.where(lane == group - 1, 0.0, 0.5).astype(F32)
    em = jnp.where((lane == 0) | (lane == group - 1), 0.5, 0.0).astype(F32)
    ym = None
    if domain_rows:
        row = iota((rows, 128), 0)
        ym = jnp.where(row == rows - 1, 0.0, 0.5).astype(F32)
        em = em + jnp.where((row == 0) | (row == rows - 1), 0.5, 0.0).astype(F32)
    return zm, em, ym


def loop(first, last, rows, step, carry):
    count = last - first
    width = max(1, min(count, UNROLL // (rows // 8)))
    whole = count // width

    def block(i, carry):
        for u in range(width):
            carry = step(first + i * width + u, carry)
        return carry

    if whole == 1:
        carry = block(0, carry)
    else:
        carry = lax.fori_loop(0, whole, block, carry)
    for p in range(first + whole * width, last):
        carry = step(p, carry)
    return carry


def make_faces(n, k, ax, ay, az, consts, inv=None, extra=None):
    zm, em, ym = consts

    def step(p, before):
        here = k[p]
        x = 0.5 * (here + k[p + 1])
        y = here + roll(here, -1, 0)
        y = 0.5 * y if ym is None else ym * y
        z = zm * (here + roll(here, -1, 1))
        ax[p] = x
        ay[p] = y
        az[p] = z
        if inv is not None:
            diag = em * here + x + before + y + roll(y, 1, 0) + z + roll(z, 1, 1)
            scaled = jnp.where(here > 0.0, OMEGA / diag, 0.0)
            inv[p] = scaled
            if extra is not None:
                extra(p, scaled)
        return x

    loop(0, n - 1, k.shape[1], step, jnp.zeros(k.shape[1:], F32))


def apply_planes(first, last, v, k, ax, ay, az, consts, use, carry=None):
    em = consts[1]

    def step(p, state):
        before, carry = state
        here = v[p]
        x = ax[p] * (here - v[p + 1])
        y = ay[p] * (here - roll(here, -1, 0))
        z = az[p] * (here - roll(here, -1, 1))
        total = em * k[p] * here + (x - before) + (y - roll(y, 1, 0)) + (z - roll(z, 1, 1))
        return x, use(p, here, total, carry)

    start = ax[first - 1] * (v[first - 1] - v[first])
    return loop(first, last, v.shape[1], step, (start, carry))[1]


def sweep(first, last, v, out, b, inv, k, ax, ay, az, consts):
    def use(p, here, total, _):
        out[p] = here + inv[p] * (b[p] - total)
        return 0

    apply_planes(first, last, v, k, ax, ay, az, consts, use, 0)


def ghosts(ref, n, width):
    lane = iota(ref.shape[1:], 1)
    ref[0] = jnp.where(lane < width, 0.0, roll(ref[n - 2], width, 1))
    ref[n - 1] = jnp.where(lane >= 128 - width, 0.0, roll(ref[1], -width, 1))


def pair_rows(tmp, x):
    half = x.shape[0] // 2
    tmp[...] = x
    return tmp[pl.ds(0, half, 2), :] + tmp[pl.ds(1, half, 2), :]


def twice_rows(tmp, x):
    n = x.shape[0]
    tmp[pl.ds(0, n, 2), :] = x
    tmp[pl.ds(1, n, 2), :] = x
    return tmp[...]


def gather_matrix(source, weight):
    return jnp.where(iota((128, 128), 0) == source(iota((128, 128), 1)), weight, 0.0).astype(F32)


def pair_matrix(target, weight):
    return jnp.where(iota((128, 128), 1) == target(iota((128, 128), 0)), weight, 0.0).astype(F32)


SENT = [(0, d, h) for d, h in zip(range(1, 9), (16, 16, 12, 12, 12, 12, 8, 0))]
SENT += [(1, d, h) for d, h in zip(range(1, 7), (16, 12, 12, 12, 12, 8))]
CORNER_ROWS = sum(2 * h for _, _, h in SENT)


def sent_plane(d, on_chip):
    return jnp.where(lax.axis_index("outer") % 2 == (0 if on_chip else 1), 8 - d, d - 1)


def prep_kernel(b_ref, codes_ref, even_ref, odd_ref, own_ref, side_ref):
    kappa = jnp.exp(0.5 * codes_ref[...].astype(F32))
    up_first = lax.axis_index("inner") % 2 == 0
    for part, field in enumerate((kappa, b_ref[...])):
        low, high = field[:, :16], field[:, 16:]
        even_ref[part] = jnp.where(up_first, high, low)
        odd_ref[part] = jnp.where(up_first, low, high)
        own_ref[part] = field
    for i, (field, d, _) in enumerate(SENT):
        side_ref[i] = own_ref[field, sent_plane(d, False)]


def pack_kernel(from_even_ref, from_odd_ref, own_ref, corner_ref, halo_ref, chip_ref):
    up_first = lax.axis_index("inner") % 2 == 0
    for field in range(2):
        for p in range(8):
            even, odd = from_even_ref[field, p], from_odd_ref[field, p]
            halo_ref[field, p, 0:16, :] = jnp.where(up_first, odd, even)
            halo_ref[field, p, 16:32, :] = jnp.where(up_first, even, odd)
    first = 0
    for i, (field, d, h) in enumerate(SENT):
        chip_ref[32 * i : 32 * i + 32, :] = own_ref[field, sent_plane(d, True)]
        if h:
            corner_ref[first : first + 2 * h, :] = halo_ref[field, sent_plane(d, False), 16 - h : 16 + h, :]
            place = 32 * len(SENT) + first
            chip_ref[place : place + 2 * h, :] = halo_ref[field, sent_plane(d, True), 16 - h : 16 + h, :]
            first += 2 * h


def fine_kernel(
    own_ref, halo_ref, chip_ref, side_ref, corner_ref,
    pay_ref, vb_ref, k1_ref, inv1_ref, k0_ref, b0_ref, v0_ref, inv0_ref,
    kb, ax, ay, az, inv, va, vb, tmp64, tmp32, s1, sk, b1, ax1, ay1, az1, va1, vb1,
):
    core = lax.axis_index("outer") % 2
    zeros = jnp.zeros((64, 128), F32)
    for place in (0, 1, 22, 23):
        kb[1, place] = zeros
    first = 0
    for i, (field, d, h) in enumerate(SENT):
        for on_chip in (False, True):
            place = jnp.where(core == (1 if on_chip else 0), 8 - d, 15 + d)
            if h < 16:
                kb[field, place, 0:16, :] = zeros[0:16]
                kb[field, place, 48:64, :] = zeros[0:16]
            kb[field, place, 16:48, :] = chip_ref[1 - core, 32 * i : 32 * i + 32, :] if on_chip else side_ref[i]
            if h:
                corners, start = (chip_ref.at[1 - core], 32 * len(SENT) + first) if on_chip else (corner_ref, first)
                kb[field, place, 16 - h : 16, :] = corners[start : start + h, :]
                kb[field, place, 48 : 48 + h, :] = corners[start + h : start + 2 * h, :]
        first += 2 * h
    for field in range(2):
        for p in range(8):
            kb[field, 8 + p, 0:16, :] = halo_ref[field, p, 0:16, :]
            kb[field, 8 + p, 16:48, :] = own_ref[field, p]
            kb[field, 8 + p, 48:64, :] = halo_ref[field, p, 16:32, :]

    k, b = kb.at[0], kb.at[1]
    consts = lane_consts(64, 128)

    def first_sweep(p, scaled):
        va[p] = scaled * b[p]

    make_faces(24, k, ax, ay, az, consts, inv, first_sweep)
    sweep(2, 22, va, vb, b, inv, k, ax, ay, az, consts)

    def keep(p, _):
        k0_ref[p] = k[p + 4, pl.ds(8, 48), :]
        b0_ref[p] = b[p + 4, pl.ds(8, 48), :]
        v0_ref[p] = vb[p + 4, pl.ds(8, 48), :]
        inv0_ref[p] = inv[p + 4, pl.ds(8, 48), :]
        return 0

    loop(0, 16, 32, keep, 0)

    def use(p, here, total, _):
        va[p] = b[p] - total
        return 0

    apply_planes(4, 20, vb, k, ax, ay, az, consts, use, 0)

    def coarsen_b(q, _):
        s1[pl.ds((q - 2) * 32, 32), :] = pair_rows(tmp64, va[2 * q] + va[2 * q + 1])
        return 0

    def coarsen_k(q, _):
        sk[pl.ds(q * 32, 32), :] = pair_rows(tmp64, k[2 * q] + k[2 * q + 1])
        return 0

    loop(2, 10, 64, coarsen_b, 0)
    loop(0, 12, 64, coarsen_k, 0)
    b1[pl.ds(2, 8)] = dot(s1[...], pair_matrix(lambda i: i // 2, 0.125)).reshape(8, 32, 128)
    k1_ref[...] = dot(sk[...], pair_matrix(lambda i: i // 2, 0.03125)).reshape(12, 32, 128)

    consts1 = lane_consts(32, 64)
    make_faces(12, k1_ref, ax1, ay1, az1, consts1, inv1_ref)
    va1[pl.ds(2, 8)] = inv1_ref[pl.ds(2, 8)] * b1[pl.ds(2, 8)]
    sweep(3, 9, va1, vb1, b1, inv1_ref, k1_ref, ax1, ay1, az1, consts1)

    def use1(p, here, total, _):
        va1[p] = b1[p] - total
        return 0

    apply_planes(4, 8, vb1, k1_ref, ax1, ay1, az1, consts1, use1, 0)
    for p in range(4):
        vb_ref[p] = vb1[4 + p] + roll(b1[4 + p], 64, 1)

    pay = jnp.zeros((16, 128), F32)
    for part, (field, weight) in enumerate(((va1, 0.125), (k1_ref, 0.03125))):
        for half in range(2):
            place = 64 * part + 32 * half
            rows = pair_rows(tmp32, field[4 + 2 * half] + field[5 + 2 * half])
            pay = pay + dot(rows, pair_matrix(lambda i: jnp.where(i < 64, place + i // 2, -1), weight))
    for i in range(32):
        pay_ref[i] = pay


def middle_kernel(
    all_ref, pay_ref, edge_ref, kw_ref, invw_ref, bw_ref, vw_ref,
    k_ref, inv_ref, b_ref, v_ref, ax, ay, az, va, vb, tmp16, s, sk,
):
    group = iota((16, 128), 1) // 32
    for xl in range(16):
        for part, field in enumerate((b_ref, k_ref)):
            place = 2 * part + xl % 2
            plane = None
            for xh in range(4):
                block = all_ref[xl // 2 + 8 * xh]
                moved = block if xh == place else roll(block, 32 * (xh - place), 1)
                plane = moved if plane is None else jnp.where(group == xh, moved, plane)
            field[xl + 1] = plane
    ghosts(k_ref, 18, 32)
    consts = lane_consts(16, 32)
    inv_ref[0] = jnp.zeros((16, 128), F32)
    inv_ref[17] = jnp.zeros((16, 128), F32)
    b_ref[0] = jnp.zeros((16, 128), F32)
    b_ref[17] = jnp.zeros((16, 128), F32)

    def first_sweep(p, scaled):
        va[p] = scaled * b_ref[p]

    make_faces(18, k_ref, ax, ay, az, consts, inv_ref, first_sweep)
    ghosts(va, 18, 32)
    sweep(1, 17, va, v_ref, b_ref, inv_ref, k_ref, ax, ay, az, consts)
    ghosts(v_ref, 18, 32)

    def use(p, here, total, _):
        vb[p] = b_ref[p] - total
        return 0

    apply_planes(1, 17, v_ref, k_ref, ax, ay, az, consts, use, 0)
    sends_b = lax.axis_index("outer") % 2 == 0
    first = 4 * (lax.axis_index("outer") // 2) + 60
    near = []
    for q in range(12):
        x = lax.rem(first + q, 64)
        place = lax.rem(x, 16) + 1
        back = lax.rem(128 - 32 * (x // 16), 128)
        kept = (group == 0) & (first + q >= 64) & (first + q < 128)
        for field, window in ((k_ref, kw_ref), (inv_ref, invw_ref), (b_ref, bw_ref), (v_ref, vw_ref)):
            window[q] = jnp.where(kept, pltpu.roll(field[place], back, 1), 0.0)
        near.append(vw_ref[q] + roll(bw_ref[q], 32, 1))
    for q in range(6):
        both = near[q] + roll(near[q + 6], 64, 1)
        edge_ref[4 * q : 4 * q + 4, :] = jnp.where(sends_b, both[8:12], both[4:8])
    for t in range(8):
        s[t] = pair_rows(tmp16, vb[2 * t + 1] + vb[2 * t + 2])
        sk[t] = pair_rows(tmp16, k_ref[2 * t + 1] + k_ref[2 * t + 2])

    small = jnp.zeros((32, 128), F32)
    for u in range(2):
        m = pair_matrix(lambda i: (i // 32) * 32 + u * 16 + (i % 32) // 2, 0.03125)
        rows = jnp.where(sends_b, 4.0 * s[pl.ds(4 * u, 4)], sk[pl.ds(4 * u, 4)])
        small = small + dot(rows.reshape(32, 128), m)
    for t in range(4):
        vb[0, 4 * t : 4 * t + 4, :] = small[8 * t + 2 : 8 * t + 6, :]
    piece = vb[0]
    for i in range(16):
        pay_ref[i] = piece


def coarse_kernel(
    half_ref, edges_ref, k2_ref, inv2_ref, b2_ref, v2_ref, odd_ref, k1_ref, inv1_ref,
    k0, b0, v0_ref, inv0, v_out, r_out,
    k3, b3, ax3, ay3, az3, inv3, va3, vb3, c3, tmp16, ax2, ay2, az2, va2, vb2, b2,
    tmp32, b1, va1, vb1, ax1, ay1, az1, tmp64, c1, v0, ax0, ay0, az0, w0,
):
    outer, inner = lax.axis_index("outer"), lax.axis_index("inner")

    for i in range(16):
        for t in range(4):
            b3[t + 1, 4 * i : 4 * i + 4, :] = half_ref[0, i, 4 * t : 4 * t + 4, :]
            k3[t + 1, 4 * i : 4 * i + 4, :] = half_ref[1, i, 4 * t : 4 * t + 4, :]
    ghosts(k3, 6, 16)
    b3[0] = jnp.zeros((64, 128), F32)
    consts3 = lane_consts(64, 16, True)

    def first_sweep(p, scaled):
        va3[p] = scaled * b3[p]

    make_faces(6, k3, ax3, ay3, az3, consts3, inv3, first_sweep)
    now, later = va3, vb3
    ghosts(now, 6, 16)
    for _ in range(5):
        sweep(1, 5, now, later, b3, inv3, k3, ax3, ay3, az3, consts3)
        now, later = later, now
        ghosts(now, 6, 16)

    def leftover(p, here, total, carry):
        return carry + (b3[p] - total)

    rest = apply_planes(1, 5, now, k3, ax3, ay3, az3, consts3, leftover, jnp.zeros((64, 128), F32))
    lane = iota((64, 128), 1)
    border = jnp.where(lane < 16, 0.5 * k3[1], 0.0) + jnp.where(lane >= 112, 0.5 * k3[4], 0.0)
    for p in range(1, 5):
        border = border + consts3[1] * k3[p]
    shift = jnp.sum(rest, keepdims=True) / jnp.sum(border, keepdims=True)
    for t in range(4):
        c3[t, 0:8, :] = jnp.zeros((8, 128), F32)
        c3[t, 8:72, :] = now[t + 1] + shift
        c3[t, 72:80, :] = jnp.zeros((8, 128), F32)

    near = []
    core = lax.rem(outer, 2)
    for q in range(6):
        x = lax.rem(outer - core + 30 + q, 32)
        back = lax.rem(128 - 16 * (x // 4), 128)
        near.append(pltpu.roll(c3[lax.rem(x, 4), pl.ds(4 * inner + 6, 8), :], back, 1))
    wide = dot(jnp.concatenate(near, axis=0), gather_matrix(lambda j: jnp.where(j < 32, j // 2, -1), 1.0))
    lane = iota((16, 128), 1)
    for q in range(12):
        rows = twice_rows(tmp16, wide[8 * (q // 2) : 8 * (q // 2) + 8])
        below, above = (edges_ref[i, 4 * (q % 6) : 4 * (q % 6) + 4, :] for i in range(2))
        if q >= 6:
            below, above = roll(below, 64, 1), roll(above, 64, 1)
        v2 = jnp.concatenate([below, v2_ref[q, 4:12, :], above], axis=0)
        b2[q] = jnp.concatenate([roll(below, 96, 1), b2_ref[q, 4:12, :], roll(above, 96, 1)], axis=0)
        va2[q] = jnp.where((lane < 32) & (k2_ref[q] > 0.0), v2 + rows, 0.0)
    consts2 = lane_consts(16, 32)
    make_faces(12, k2_ref, ax2, ay2, az2, consts2)
    sweep(1, 11, va2, vb2, b2, inv2_ref, k2_ref, ax2, ay2, az2, consts2)
    sweep(2, 10, vb2, va2, b2, inv2_ref, k2_ref, ax2, ay2, az2, consts2)

    wide = dot(va2[pl.ds(2 + 2 * core, 6)].reshape(96, 128), gather_matrix(lambda j: jnp.where(j < 64, j // 2, -1), 1.0))
    left_is_odd = outer % 2 == 0
    low = iota((32, 128), 1) < 64
    for q in range(6):
        rows = twice_rows(tmp32, wide[16 * q : 16 * q + 16])
        for p in (2 * q, 2 * q + 1):
            first, second = (edges_ref[i, 24 + 32 * (p % 4) : 56 + 32 * (p % 4), :] for i in range(2))
            if p < 4:
                both = jnp.where(left_is_odd, odd_ref[p], first)
            elif p < 8:
                both = jnp.where(left_is_odd, first, second)
            else:
                both = jnp.where(left_is_odd, second, odd_ref[p - 8])
            b1[p] = roll(both, 64, 1)
            va1[p] = jnp.where(low & (k1_ref[p] > 0.0), both + rows, 0.0)
    consts1 = lane_consts(32, 64)
    make_faces(12, k1_ref, ax1, ay1, az1, consts1)
    sweep(1, 11, va1, vb1, b1, inv1_ref, k1_ref, ax1, ay1, az1, consts1)
    sweep(2, 10, vb1, va1, b1, inv1_ref, k1_ref, ax1, ay1, az1, consts1)

    c1[...] = dot(va1[pl.ds(2, 8)].reshape(256, 128), gather_matrix(lambda j: j // 2, 1.0))

    def correct(q, _):
        twice_rows(tmp64, c1[pl.ds(32 * q, 32), :])
        rows = tmp64[pl.ds(8, 48), :]
        for p in (2 * q, 2 * q + 1):
            v0[p] = jnp.where(k0[p] > 0.0, v0_ref[p] + rows, 0.0)
        return 0

    loop(0, 8, 64, correct, 0)
    consts0 = lane_consts(48, 128)
    make_faces(16, k0, ax0, ay0, az0, consts0)
    sweep(2, 14, v0, w0, b0, inv0, k0, ax0, ay0, az0, consts0)
    sweep(3, 13, w0, v0, b0, inv0, k0, ax0, ay0, az0, consts0)

    def use(p, here, total, _):
        v_out[p - 4] = here[8:40]
        r_out[p - 4] = (b0[p] - total)[8:40]
        return 0

    apply_planes(4, 12, v0, k0, ax0, ay0, az0, consts0, use, 0)


def vmem(*shape):
    return pltpu.VMEM(shape, F32)


def out(*shape):
    return jax.ShapeDtypeStruct(shape, F32)


def call(kernel, name, ins, outs, scratch, args):
    spec = {"v": pl.BlockSpec(memory_space=pltpu.VMEM), "a": pl.BlockSpec(memory_space=pl.ANY)}
    return pl.pallas_call(
        kernel,
        name=name,
        out_shape=outs,
        in_specs=[spec[c] for c in ins],
        out_specs=[spec["v"]] * len(outs),
        scratch_shapes=scratch,
        compiler_params=pltpu.CompilerParams(vmem_limit_bytes=VMEM_LIMIT),
    )(*args)


def body(right_side, codes):
    groups, boxes = lax.axis_size("outer"), lax.axis_size("inner")
    odds = [(i, ((i + 1) ^ 1) - 1) for i in range(1, groups - 1)]
    evens_y = [(i, i ^ 1) for i in range(boxes)]
    odds_y = [(i, ((i + 1) ^ 1) - 1) for i in range(1, boxes - 1)]

    def on_chip(x):
        return lax.all_gather(x, "outer", axis_index_groups=[[i, i + 1] for i in range(0, groups, 2)])

    to_even, to_odd, own, side = call(
        prep_kernel, "prep", "vv",
        [out(2, 8, 16, 128)] * 2 + [out(2, 8, 32, 128), out(len(SENT), 32, 128)], [], (right_side, codes),
    )
    from_even = lax.ppermute(to_even, "inner", evens_y)
    from_odd = lax.ppermute(to_odd, "inner", odds_y)
    side = lax.ppermute(side, "outer", odds)
    corner, halo, chip = call(
        pack_kernel, "pack", "vvv",
        [out(CORNER_ROWS, 128), out(2, 8, 32, 128), out(32 * len(SENT) + CORNER_ROWS, 128)], [],
        (from_even, from_odd, own),
    )
    corner = lax.ppermute(corner, "outer", odds)
    chip = on_chip(chip)

    fine, level1 = (24, 64, 128), (12, 32, 128)
    pay, vb1, k1, inv1, k0, b0, v0, inv0 = call(
        fine_kernel, "fine", "vvvvv",
        [out(32, 16, 128), out(4, 32, 128), out(*level1), out(*level1)] + [out(16, 48, 128)] * 4,
        [vmem(2, *fine)] + [vmem(*fine)] * 6 + [vmem(64, 128), vmem(32, 128), vmem(256, 128), vmem(384, 128)]
        + [vmem(*level1)] * 6,
        (own, halo, chip, side, corner),
    )
    slab = lax.all_to_all(pay, "outer", 0, 0, tiled=True)

    level2, window2 = (18, 16, 128), (12, 16, 128)
    pay3, edge, k2, inv2, b2, v2 = call(
        middle_kernel, "middle", "v",
        [out(16, 16, 128), out(24, 128)] + [out(*window2)] * 4,
        [vmem(*level2)] * 9 + [vmem(16, 128), vmem(8, 8, 128), vmem(8, 8, 128)],
        (slab,),
    )
    ups = [(i * boxes + j, i * boxes + j + 1) for i in range(0, groups, 2) for j in range(boxes - 1)]
    downs = [(i * boxes + j + 1, i * boxes + j) for i in range(1, groups, 2) for j in range(boxes - 1)]
    vb1, edge = lax.optimization_barrier((vb1, edge))
    odd1 = lax.ppermute(vb1, "outer", odds)
    edge = lax.ppermute(edge, ("outer", "inner"), ups + downs)
    half = lax.all_to_all(pay3, "inner", 0, 0, tiled=True)
    edges = on_chip(jnp.concatenate([edge, vb1.reshape(128, 128)], axis=0))
    half, edges = lax.optimization_barrier((half, edges))

    level3, window = (6, 64, 128), (16, 48, 128)
    return call(
        coarse_kernel, "coarse", "v" * 13,
        [out(8, 32, 128)] * 2,
        [vmem(*level3)] * 8 + [vmem(4, 80, 128), vmem(16, 128)] + [vmem(*window2)] * 6
        + [vmem(32, 128)] + [vmem(*level1)] * 6 + [vmem(64, 128), vmem(256, 128)]
        + [vmem(*window)] * 5,
        (on_chip(half), edges, k2, inv2, b2, v2, odd1, k1, inv1, k0, b0, v0, inv0),
    )


def solution(mesh):
    placed = P("outer", "inner", None)
    return jax.shard_map(
        lambda right_side, codes: tuple(body(right_side, codes)),
        mesh=mesh,
        in_specs=(placed, placed),
        out_specs=(placed, placed),
        check_vma=False,
    )
```

```python
import jax
import jax.numpy as jnp
from jax import lax
from jax.experimental import pallas as pl
from jax.experimental.pallas import tpu as pltpu
from jax.sharding import PartitionSpec as P


OMEGA = 0.8
F32 = jnp.float32
VMEM_LIMIT = 24 * 1024 * 1024
UNROLL = 96


def iota(shape, dim):
    return lax.broadcasted_iota(jnp.int32, shape, dim)


def roll(x, shift, axis):
    return pltpu.roll(x, shift % x.shape[axis], axis)


def dot(a, b):
    b = b.astype(jnp.bfloat16)
    total = None
    for _ in range(3):
        part = a.astype(jnp.bfloat16)
        a = a - part.astype(F32)
        product = jnp.dot(part, b, preferred_element_type=F32)
        total = product if total is None else total + product
    return total


def lane_consts(rows, group, domain_rows=False):
    lane = iota((rows, 128), 1) % group
    zm = jnp.where(lane == group - 1, 0.0, 0.5).astype(F32)
    em = jnp.where((lane == 0) | (lane == group - 1), 0.5, 0.0).astype(F32)
    ym = None
    if domain_rows:
        row = iota((rows, 128), 0)
        ym = jnp.where(row == rows - 1, 0.0, 0.5).astype(F32)
        em = em + jnp.where((row == 0) | (row == rows - 1), 0.5, 0.0).astype(F32)
    return zm, em, ym


def loop(first, last, rows, step, carry):
    count = last - first
    width = max(1, min(count, UNROLL // (rows // 8)))
    whole = count // width

    def block(i, carry):
        for u in range(width):
            carry = step(first + i * width + u, carry)
        return carry

    if whole == 1:
        carry = block(0, carry)
    else:
        carry = lax.fori_loop(0, whole, block, carry)
    for p in range(first + whole * width, last):
        carry = step(p, carry)
    return carry


def make_faces(n, k, ax, ay, az, consts, inv=None, extra=None):
    zm, em, ym = consts

    def step(p, before):
        here = k[p]
        x = 0.5 * (here + k[p + 1])
        y = here + roll(here, -1, 0)
        y = 0.5 * y if ym is None else ym * y
        z = zm * (here + roll(here, -1, 1))
        ax[p] = x
        ay[p] = y
        az[p] = z
        if inv is not None:
            diag = em * here + x + before + y + roll(y, 1, 0) + z + roll(z, 1, 1)
            scaled = jnp.where(here > 0.0, OMEGA / diag, 0.0)
            inv[p] = scaled
            if extra is not None:
                extra(p, scaled)
        return x

    loop(0, n - 1, k.shape[1], step, jnp.zeros(k.shape[1:], F32))


def apply_planes(first, last, v, k, ax, ay, az, consts, use, carry=None):
    em = consts[1]

    def step(p, state):
        before, carry = state
        here = v[p]
        x = ax[p] * (here - v[p + 1])
        y = ay[p] * (here - roll(here, -1, 0))
        z = az[p] * (here - roll(here, -1, 1))
        total = em * k[p] * here + (x - before) + (y - roll(y, 1, 0)) + (z - roll(z, 1, 1))
        return x, use(p, here, total, carry)

    start = ax[first - 1] * (v[first - 1] - v[first])
    return loop(first, last, v.shape[1], step, (start, carry))[1]


def sweep(first, last, v, out, b, inv, k, ax, ay, az, consts):
    def use(p, here, total, _):
        out[p] = here + inv[p] * (b[p] - total)
        return 0

    apply_planes(first, last, v, k, ax, ay, az, consts, use, 0)


def ghosts(ref, n, width):
    lane = iota(ref.shape[1:], 1)
    ref[0] = jnp.where(lane < width, 0.0, roll(ref[n - 2], width, 1))
    ref[n - 1] = jnp.where(lane >= 128 - width, 0.0, roll(ref[1], -width, 1))


def pair_rows(tmp, x):
    half = x.shape[0] // 2
    tmp[...] = x
    return tmp[pl.ds(0, half, 2), :] + tmp[pl.ds(1, half, 2), :]


def twice_rows(tmp, x):
    n = x.shape[0]
    tmp[pl.ds(0, n, 2), :] = x
    tmp[pl.ds(1, n, 2), :] = x
    return tmp[...]


def gather_matrix(source, weight):
    return jnp.where(iota((128, 128), 0) == source(iota((128, 128), 1)), weight, 0.0).astype(F32)


def pair_matrix(target, weight):
    return jnp.where(iota((128, 128), 1) == target(iota((128, 128), 0)), weight, 0.0).astype(F32)


SENT = [(0, d, h) for d, h in zip(range(1, 9), (14, 14, 12, 12, 10, 10, 8, 0))]
SENT += [(1, d, h) for d, h in zip(range(1, 7), (14, 12, 12, 10, 10, 8))]
CORNER_ROWS = sum(2 * h for _, _, h in SENT)


def sent_plane(d, on_chip):
    return jnp.where(lax.axis_index("outer") % 2 == (0 if on_chip else 1), 8 - d, d - 1)


def prep_kernel(b_ref, codes_ref, even_ref, odd_ref, own_ref, side_ref):
    kappa = jnp.exp(0.5 * codes_ref[...].astype(F32))
    up_first = lax.axis_index("inner") % 2 == 0
    for part, field in enumerate((kappa, b_ref[...])):
        low, high = field[:, :16], field[:, 16:]
        even_ref[part] = jnp.where(up_first, high, low)
        odd_ref[part] = jnp.where(up_first, low, high)
        own_ref[part] = field
    for i, (field, d, _) in enumerate(SENT):
        side_ref[i] = own_ref[field, sent_plane(d, False)]


def pack_kernel(from_even_ref, from_odd_ref, own_ref, corner_ref, halo_ref, chip_ref):
    up_first = lax.axis_index("inner") % 2 == 0
    for field in range(2):
        for p in range(8):
            even, odd = from_even_ref[field, p], from_odd_ref[field, p]
            halo_ref[field, p, 0:16, :] = jnp.where(up_first, odd, even)
            halo_ref[field, p, 16:32, :] = jnp.where(up_first, even, odd)
    first = 0
    for i, (field, d, h) in enumerate(SENT):
        chip_ref[32 * i : 32 * i + 32, :] = own_ref[field, sent_plane(d, True)]
        if h:
            corner_ref[first : first + 2 * h, :] = halo_ref[field, sent_plane(d, False), 16 - h : 16 + h, :]
            place = 32 * len(SENT) + first
            chip_ref[place : place + 2 * h, :] = halo_ref[field, sent_plane(d, True), 16 - h : 16 + h, :]
            first += 2 * h


def fine_kernel(
    own_ref, halo_ref, chip_ref, side_ref, corner_ref,
    pay_ref, vb_ref, k1_ref, inv1_ref, k0_ref, b0_ref, v0_ref, inv0_ref,
    kb, ax, ay, az, inv, va, vb, tmp64, tmp32, s1, sk, b1, ax1, ay1, az1, va1, vb1,
):
    core = lax.axis_index("outer") % 2
    zeros = jnp.zeros((64, 128), F32)
    for place in (0, 1, 22, 23):
        kb[1, place] = zeros
    first = 0
    for i, (field, d, h) in enumerate(SENT):
        for on_chip in (False, True):
            place = jnp.where(core == (1 if on_chip else 0), 8 - d, 15 + d)
            if h < 16:
                kb[field, place, 0:16, :] = zeros[0:16]
                kb[field, place, 48:64, :] = zeros[0:16]
            kb[field, place, 16:48, :] = chip_ref[1 - core, 32 * i : 32 * i + 32, :] if on_chip else side_ref[i]
            if h:
                corners, start = (chip_ref.at[1 - core], 32 * len(SENT) + first) if on_chip else (corner_ref, first)
                kb[field, place, 16 - h : 16, :] = corners[start : start + h, :]
                kb[field, place, 48 : 48 + h, :] = corners[start + h : start + 2 * h, :]
        first += 2 * h
    for field in range(2):
        for p in range(8):
            kb[field, 8 + p, 0:16, :] = halo_ref[field, p, 0:16, :]
            kb[field, 8 + p, 16:48, :] = own_ref[field, p]
            kb[field, 8 + p, 48:64, :] = halo_ref[field, p, 16:32, :]

    k, b = kb.at[0], kb.at[1]
    consts = lane_consts(64, 128)

    def first_sweep(p, scaled):
        va[p] = scaled * b[p]

    make_faces(24, k, ax, ay, az, consts, inv, first_sweep)
    sweep(2, 22, va, vb, b, inv, k, ax, ay, az, consts)

    def keep(p, _):
        k0_ref[p] = k[p + 4, pl.ds(8, 48), :]
        b0_ref[p] = b[p + 4, pl.ds(8, 48), :]
        v0_ref[p] = vb[p + 4, pl.ds(8, 48), :]
        inv0_ref[p] = inv[p + 4, pl.ds(8, 48), :]
        return 0

    loop(0, 16, 32, keep, 0)

    def use(p, here, total, _):
        va[p] = b[p] - total
        return 0

    apply_planes(4, 20, vb, k, ax, ay, az, consts, use, 0)

    def coarsen_b(q, _):
        s1[pl.ds((q - 2) * 32, 32), :] = pair_rows(tmp64, va[2 * q] + va[2 * q + 1])
        return 0

    def coarsen_k(q, _):
        sk[pl.ds(q * 32, 32), :] = pair_rows(tmp64, k[2 * q] + k[2 * q + 1])
        return 0

    loop(2, 10, 64, coarsen_b, 0)
    loop(0, 12, 64, coarsen_k, 0)
    b1[pl.ds(2, 8)] = dot(s1[...], pair_matrix(lambda i: i // 2, 0.125)).reshape(8, 32, 128)
    k1_ref[...] = dot(sk[...], pair_matrix(lambda i: i // 2, 0.03125)).reshape(12, 32, 128)

    consts1 = lane_consts(32, 64)
    make_faces(12, k1_ref, ax1, ay1, az1, consts1, inv1_ref)
    va1[pl.ds(2, 8)] = inv1_ref[pl.ds(2, 8)] * b1[pl.ds(2, 8)]
    sweep(3, 9, va1, vb1, b1, inv1_ref, k1_ref, ax1, ay1, az1, consts1)

    def use1(p, here, total, _):
        va1[p] = b1[p] - total
        return 0

    apply_planes(4, 8, vb1, k1_ref, ax1, ay1, az1, consts1, use1, 0)
    for p in range(4):
        vb_ref[p] = vb1[4 + p] + roll(b1[4 + p], 64, 1)

    pay = jnp.zeros((16, 128), F32)
    for part, (field, weight) in enumerate(((va1, 0.125), (k1_ref, 0.03125))):
        for half in range(2):
            place = 64 * part + 32 * half
            rows = pair_rows(tmp32, field[4 + 2 * half] + field[5 + 2 * half])
            pay = pay + dot(rows, pair_matrix(lambda i: jnp.where(i < 64, place + i // 2, -1), weight))
    for i in range(32):
        pay_ref[i] = pay


def middle_kernel(
    all_ref, pay_ref, edge_ref, kw_ref, invw_ref, bw_ref, vw_ref,
    k_ref, inv_ref, b_ref, v_ref, ax, ay, az, va, vb, tmp16, s, sk,
):
    group = iota((16, 128), 1) // 32
    for xl in range(16):
        for part, field in enumerate((b_ref, k_ref)):
            place = 2 * part + xl % 2
            plane = None
            for xh in range(4):
                block = all_ref[xl // 2 + 8 * xh]
                moved = block if xh == place else roll(block, 32 * (xh - place), 1)
                plane = moved if plane is None else jnp.where(group == xh, moved, plane)
            field[xl + 1] = plane
    ghosts(k_ref, 18, 32)
    consts = lane_consts(16, 32)
    inv_ref[0] = jnp.zeros((16, 128), F32)
    inv_ref[17] = jnp.zeros((16, 128), F32)
    b_ref[0] = jnp.zeros((16, 128), F32)
    b_ref[17] = jnp.zeros((16, 128), F32)

    def first_sweep(p, scaled):
        va[p] = scaled * b_ref[p]

    make_faces(18, k_ref, ax, ay, az, consts, inv_ref, first_sweep)
    ghosts(va, 18, 32)
    sweep(1, 17, va, v_ref, b_ref, inv_ref, k_ref, ax, ay, az, consts)
    ghosts(v_ref, 18, 32)

    def use(p, here, total, _):
        vb[p] = b_ref[p] - total
        return 0

    apply_planes(1, 17, v_ref, k_ref, ax, ay, az, consts, use, 0)
    sends_b = lax.axis_index("outer") % 2 == 0
    first = 4 * (lax.axis_index("outer") // 2) + 60
    near = []
    for q in range(12):
        x = lax.rem(first + q, 64)
        place = lax.rem(x, 16) + 1
        back = lax.rem(128 - 32 * (x // 16), 128)
        kept = (group == 0) & (first + q >= 64) & (first + q < 128)
        for field, window in ((k_ref, kw_ref), (inv_ref, invw_ref), (b_ref, bw_ref), (v_ref, vw_ref)):
            window[q] = jnp.where(kept, pltpu.roll(field[place], back, 1), 0.0)
        near.append(vw_ref[q] + roll(bw_ref[q], 32, 1))
    for q in range(6):
        both = near[q] + roll(near[q + 6], 64, 1)
        edge_ref[4 * q : 4 * q + 4, :] = jnp.where(sends_b, both[8:12], both[4:8])
    for t in range(8):
        s[t] = pair_rows(tmp16, vb[2 * t + 1] + vb[2 * t + 2])
        sk[t] = pair_rows(tmp16, k_ref[2 * t + 1] + k_ref[2 * t + 2])

    small = jnp.zeros((32, 128), F32)
    for u in range(2):
        m = pair_matrix(lambda i: (i // 32) * 32 + u * 16 + (i % 32) // 2, 0.03125)
        rows = jnp.where(sends_b, 4.0 * s[pl.ds(4 * u, 4)], sk[pl.ds(4 * u, 4)])
        small = small + dot(rows.reshape(32, 128), m)
    for t in range(4):
        vb[0, 4 * t : 4 * t + 4, :] = small[8 * t + 2 : 8 * t + 6, :]
    piece = vb[0]
    for i in range(16):
        pay_ref[i] = piece


def coarse_kernel(
    half_ref, edges_ref, k2_ref, inv2_ref, b2_ref, v2_ref, odd_ref, k1_ref, inv1_ref,
    k0, b0, v0_ref, inv0, v_out, r_out,
    k3, b3, ax3, ay3, az3, inv3, va3, vb3, c3, tmp16, ax2, ay2, az2, va2, vb2, b2,
    tmp32, b1, va1, vb1, ax1, ay1, az1, tmp64, c1, v0, ax0, ay0, az0, w0,
):
    outer, inner = lax.axis_index("outer"), lax.axis_index("inner")

    for i in range(16):
        for t in range(4):
            b3[t + 1, 4 * i : 4 * i + 4, :] = half_ref[0, i, 4 * t : 4 * t + 4, :]
            k3[t + 1, 4 * i : 4 * i + 4, :] = half_ref[1, i, 4 * t : 4 * t + 4, :]
    ghosts(k3, 6, 16)
    b3[0] = jnp.zeros((64, 128), F32)
    consts3 = lane_consts(64, 16, True)

    def first_sweep(p, scaled):
        va3[p] = scaled * b3[p]

    make_faces(6, k3, ax3, ay3, az3, consts3, inv3, first_sweep)
    now, later = va3, vb3
    ghosts(now, 6, 16)
    for _ in range(5):
        sweep(1, 5, now, later, b3, inv3, k3, ax3, ay3, az3, consts3)
        now, later = later, now
        ghosts(now, 6, 16)

    def leftover(p, here, total, carry):
        return carry + (b3[p] - total)

    rest = apply_planes(1, 5, now, k3, ax3, ay3, az3, consts3, leftover, jnp.zeros((64, 128), F32))
    lane = iota((64, 128), 1)
    border = jnp.where(lane < 16, 0.5 * k3[1], 0.0) + jnp.where(lane >= 112, 0.5 * k3[4], 0.0)
    for p in range(1, 5):
        border = border + consts3[1] * k3[p]
    shift = jnp.sum(rest, keepdims=True) / jnp.sum(border, keepdims=True)
    for t in range(4):
        c3[t, 0:8, :] = jnp.zeros((8, 128), F32)
        c3[t, 8:72, :] = now[t + 1] + shift
        c3[t, 72:80, :] = jnp.zeros((8, 128), F32)

    near = []
    core = lax.rem(outer, 2)
    for q in range(6):
        x = lax.rem(outer - core + 30 + q, 32)
        back = lax.rem(128 - 16 * (x // 4), 128)
        near.append(pltpu.roll(c3[lax.rem(x, 4), pl.ds(4 * inner + 6, 8), :], back, 1))
    wide = dot(jnp.concatenate(near, axis=0), gather_matrix(lambda j: jnp.where(j < 32, j // 2, -1), 1.0))
    lane = iota((16, 128), 1)
    for q in range(12):
        rows = twice_rows(tmp16, wide[8 * (q // 2) : 8 * (q // 2) + 8])
        below, above = (edges_ref[i, 4 * (q % 6) : 4 * (q % 6) + 4, :] for i in range(2))
        if q >= 6:
            below, above = roll(below, 64, 1), roll(above, 64, 1)
        v2 = jnp.concatenate([below, v2_ref[q, 4:12, :], above], axis=0)
        b2[q] = jnp.concatenate([roll(below, 96, 1), b2_ref[q, 4:12, :], roll(above, 96, 1)], axis=0)
        va2[q] = jnp.where((lane < 32) & (k2_ref[q] > 0.0), v2 + rows, 0.0)
    consts2 = lane_consts(16, 32)
    make_faces(12, k2_ref, ax2, ay2, az2, consts2)
    sweep(1, 11, va2, vb2, b2, inv2_ref, k2_ref, ax2, ay2, az2, consts2)
    sweep(2, 10, vb2, va2, b2, inv2_ref, k2_ref, ax2, ay2, az2, consts2)

    wide = dot(va2[pl.ds(2 + 2 * core, 6)].reshape(96, 128), gather_matrix(lambda j: jnp.where(j < 64, j // 2, -1), 1.0))
    left_is_odd = outer % 2 == 0
    low = iota((32, 128), 1) < 64
    for q in range(6):
        rows = twice_rows(tmp32, wide[16 * q : 16 * q + 16])
        for p in (2 * q, 2 * q + 1):
            first, second = (edges_ref[i, 24 + 32 * (p % 4) : 56 + 32 * (p % 4), :] for i in range(2))
            if p < 4:
                both = jnp.where(left_is_odd, odd_ref[p], first)
            elif p < 8:
                both = jnp.where(left_is_odd, first, second)
            else:
                both = jnp.where(left_is_odd, second, odd_ref[p - 8])
            b1[p] = roll(both, 64, 1)
            va1[p] = jnp.where(low & (k1_ref[p] > 0.0), both + rows, 0.0)
    consts1 = lane_consts(32, 64)
    make_faces(12, k1_ref, ax1, ay1, az1, consts1)
    sweep(1, 11, va1, vb1, b1, inv1_ref, k1_ref, ax1, ay1, az1, consts1)
    sweep(2, 10, vb1, va1, b1, inv1_ref, k1_ref, ax1, ay1, az1, consts1)

    c1[...] = dot(va1[pl.ds(2, 8)].reshape(256, 128), gather_matrix(lambda j: j // 2, 1.0))

    def correct(q, _):
        twice_rows(tmp64, c1[pl.ds(32 * q, 32), :])
        rows = tmp64[pl.ds(8, 48), :]
        for p in (2 * q, 2 * q + 1):
            v0[p] = jnp.where(k0[p] > 0.0, v0_ref[p] + rows, 0.0)
        return 0

    loop(0, 8, 64, correct, 0)
    consts0 = lane_consts(48, 128)
    make_faces(16, k0, ax0, ay0, az0, consts0)
    sweep(2, 14, v0, w0, b0, inv0, k0, ax0, ay0, az0, consts0)
    sweep(3, 13, w0, v0, b0, inv0, k0, ax0, ay0, az0, consts0)

    def use(p, here, total, _):
        v_out[p - 4] = here[8:40]
        r_out[p - 4] = (b0[p] - total)[8:40]
        return 0

    apply_planes(4, 12, v0, k0, ax0, ay0, az0, consts0, use, 0)


def vmem(*shape):
    return pltpu.VMEM(shape, F32)


def out(*shape):
    return jax.ShapeDtypeStruct(shape, F32)


def call(kernel, name, ins, outs, scratch, args):
    spec = {"v": pl.BlockSpec(memory_space=pltpu.VMEM), "a": pl.BlockSpec(memory_space=pl.ANY)}
    return pl.pallas_call(
        kernel,
        name=name,
        out_shape=outs,
        in_specs=[spec[c] for c in ins],
        out_specs=[spec["v"]] * len(outs),
        scratch_shapes=scratch,
        compiler_params=pltpu.CompilerParams(vmem_limit_bytes=VMEM_LIMIT),
    )(*args)


def body(right_side, codes):
    groups, boxes = lax.axis_size("outer"), lax.axis_size("inner")
    odds = [(i, ((i + 1) ^ 1) - 1) for i in range(1, groups - 1)]
    evens_y = [(i, i ^ 1) for i in range(boxes)]
    odds_y = [(i, ((i + 1) ^ 1) - 1) for i in range(1, boxes - 1)]

    def on_chip(x):
        return lax.all_gather(x, "outer", axis_index_groups=[[i, i + 1] for i in range(0, groups, 2)])

    to_even, to_odd, own, side = call(
        prep_kernel, "prep", "vv",
        [out(2, 8, 16, 128)] * 2 + [out(2, 8, 32, 128), out(len(SENT), 32, 128)], [], (right_side, codes),
    )
    from_even = lax.ppermute(to_even, "inner", evens_y)
    from_odd = lax.ppermute(to_odd, "inner", odds_y)
    side = lax.ppermute(side, "outer", odds)
    corner, halo, chip = call(
        pack_kernel, "pack", "vvv",
        [out(CORNER_ROWS, 128), out(2, 8, 32, 128), out(32 * len(SENT) + CORNER_ROWS, 128)], [],
        (from_even, from_odd, own),
    )
    corner = lax.ppermute(corner, "outer", odds)
    chip = on_chip(chip)

    fine, level1 = (24, 64, 128), (12, 32, 128)
    pay, vb1, k1, inv1, k0, b0, v0, inv0 = call(
        fine_kernel, "fine", "vvvvv",
        [out(32, 16, 128), out(4, 32, 128), out(*level1), out(*level1)] + [out(16, 48, 128)] * 4,
        [vmem(2, *fine)] + [vmem(*fine)] * 6 + [vmem(64, 128), vmem(32, 128), vmem(256, 128), vmem(384, 128)]
        + [vmem(*level1)] * 6,
        (own, halo, chip, side, corner),
    )
    slab = lax.all_to_all(pay, "outer", 0, 0, tiled=True)

    level2, window2 = (18, 16, 128), (12, 16, 128)
    pay3, edge, k2, inv2, b2, v2 = call(
        middle_kernel, "middle", "v",
        [out(16, 16, 128), out(24, 128)] + [out(*window2)] * 4,
        [vmem(*level2)] * 9 + [vmem(16, 128), vmem(8, 8, 128), vmem(8, 8, 128)],
        (slab,),
    )
    ups = [(i * boxes + j, i * boxes + j + 1) for i in range(0, groups, 2) for j in range(boxes - 1)]
    downs = [(i * boxes + j + 1, i * boxes + j) for i in range(1, groups, 2) for j in range(boxes - 1)]
    vb1, edge = lax.optimization_barrier((vb1, edge))
    odd1 = lax.ppermute(vb1, "outer", odds)
    edge = lax.ppermute(edge, ("outer", "inner"), ups + downs)
    half = lax.all_to_all(pay3, "inner", 0, 0, tiled=True)
    edges = on_chip(jnp.concatenate([edge, vb1.reshape(128, 128)], axis=0))
    half, edges = lax.optimization_barrier((half, edges))

    level3, window = (6, 64, 128), (16, 48, 128)
    return call(
        coarse_kernel, "coarse", "v" * 13,
        [out(8, 32, 128)] * 2,
        [vmem(*level3)] * 8 + [vmem(4, 80, 128), vmem(16, 128)] + [vmem(*window2)] * 6
        + [vmem(32, 128)] + [vmem(*level1)] * 6 + [vmem(64, 128), vmem(256, 128)]
        + [vmem(*window)] * 5,
        (on_chip(half), edges, k2, inv2, b2, v2, odd1, k1, inv1, k0, b0, v0, inv0),
    )


def solution(mesh):
    placed = P("outer", "inner", None)
    return jax.shard_map(
        lambda right_side, codes: tuple(body(right_side, codes)),
        mesh=mesh,
        in_specs=(placed, placed),
        out_specs=(placed, placed),
        check_vma=False,
    )
```
